512 devices in a mesh: tiles: 128 (over z, y, core), sub: 4 (over x).
Axes of the slice: x: 4, y: 8, z: 8, core: 2. Of those that a mesh axis runs over, the one named last changes fastest.
Arguments:
- state: float32 [80, 3, 8, 512, 128], P(None, None, 'sub', 'tiles'), may hold values from -6 to 6
- eastward_current: float32 [8, 128], P('sub'), may hold values from -0.3 to 0.3
- northward_current: float32 [8, 128], P('sub'), may hold values from -0.3 to 0.3
- obs_col: int32 [12, 128], replicated, may hold values from 0 to 511, as said below
- obs_row: int32 [12, 128], replicated, may hold values from 0 to 127
- obs_field: int32 [12, 128], replicated, may hold values from 0 to 2
- obs_class: int32 [12, 128], replicated, may hold values from 0 to 3
- obs_value: float32 [12, 128], replicated, may hold values from -6 to 6
- obs_error: float32 [12, 128], replicated, may hold values from 0.02 to 0.3
- vertical_table: float32 [4, 8], P(None, 'sub'), may hold values from 0.1 to 1
Outputs:
- analysis: float32 [80, 3, 8, 512, 128], P(None, None, 'sub', 'tiles')
The draws below stay inside these ranges and needn't reach their ends.
Inputs may be any that keep to these rules, and one draw needn't show every extreme that they name: `obs_col`: the observations of one batch lie in 4 consecutive column tiles of 4 columns each, counted cyclically from a tile drawn for the batch.
All inputs are finite; a program needn't handle non-finite values.
Results may differ from the reference program's by a relative error of at most 0.00014.
Values sent between devices are 32-bit elements; how exact they have to be, the bound alone decides.
No kernel may reach another device: no remote copies, remote signals or barrier semaphores. Data moves between devices by JAX's collectives and lax.ppermute only.
A program may use at most 64 MiB of HBM per device.

```python
import math
import jax
import jax.numpy as jnp
from jax import lax

MEMBERS = 80
FIELDS = 3
CX = 4
NY = 128
OBS = 128
NBATCH = 12
NCLASS = 4
FOOT = 4
RADY = 40
LEV = 8
NX = 512
RADX = 512
N_TILES = 128


def draw_obs_col(key, part):
    anchor = jax.random.randint(jax.random.fold_in(key, 11), (NBATCH, 1), 0, N_TILES)
    offset = jax.random.randint(jax.random.fold_in(key, 12), (NBATCH, OBS), 0, FOOT * CX)
    return ((anchor * CX + offset) % NX).astype(jnp.int32)


def plant(values, stream_key, least, largest):
    extent = values.shape
    place = [jax.random.randint(jax.random.fold_in(stream_key, axis), (), 0, extent[axis]) for axis in range(len(extent))]
    values = values.at[tuple(place)].set(least)
    longest = extent.index(max(extent))
    place[longest] = (place[longest] + 1) % extent[longest]
    return values.at[tuple(place)].set(largest)


def shard_levels(rng, shape, shards, smallest, top_value):
    gain, own = 1.0, jax.random.fold_in(rng, 6)
    for dim, parts in shards:
        heights = jnp.exp(jax.random.uniform(jax.random.fold_in(own, dim), (parts,), jnp.float32, smallest / len(shards), top_value / len(shards)))
        gain = gain * jnp.repeat(heights, shape[dim] // parts).reshape([-1 if axis == dim else 1 for axis in range(len(shape))])
    return gain


def gaussian(own_key, dims, scale, limit, pieces=(), kind=jnp.bfloat16):
    level = shard_levels(own_key, dims, pieces, -0.22, 0.18) if pieces else 1.0
    drawn = jax.random.normal(own_key, dims, jnp.float32) * scale * level
    return jnp.minimum(jnp.maximum(drawn, -limit), limit).astype(kind)


def setup_inputs(seed: int = 0) -> dict:
    arg_keys = jax.random.split(jax.random.key(seed), 11)
    state = gaussian(arg_keys[0], (MEMBERS, FIELDS, LEV, NX, NY), 1.0, 6.0, ((2, 4), (3, 128)), jnp.float32)
    eastward_current = jnp.clip(jax.random.uniform(arg_keys[1], (LEV, NY), jnp.float32, -0.3, 0.3) * shard_levels(arg_keys[1], (LEV, NY), ((0, 4),), -0.4, 0.0), -0.3, 0.3)
    northward_current = jnp.clip(jax.random.uniform(arg_keys[2], (LEV, NY), jnp.float32, -0.3, 0.3) * shard_levels(arg_keys[2], (LEV, NY), ((0, 4),), -0.4, 0.0), -0.3, 0.3)
    obs_col = draw_obs_col(jax.random.fold_in(arg_keys[10], 71), 0)
    obs_row = plant(jax.random.randint(arg_keys[4], (NBATCH, OBS), 0, NY), jax.random.fold_in(arg_keys[4], 1), 0, NY - 1).astype(jnp.int32)
    obs_field = plant(jax.random.randint(arg_keys[5], (NBATCH, OBS), 0, FIELDS), jax.random.fold_in(arg_keys[5], 1), 0, FIELDS - 1).astype(jnp.int32)
    obs_class = plant(jax.random.randint(arg_keys[6], (NBATCH, OBS), 0, NCLASS), jax.random.fold_in(arg_keys[6], 1), 0, NCLASS - 1).astype(jnp.int32)
    obs_value = gaussian(arg_keys[7], (NBATCH, OBS), 1.0, 6.0, (), jnp.float32)
    obs_error = jnp.clip(jnp.exp(jax.random.uniform(arg_keys[8], (NBATCH, OBS), jnp.float32, math.log(0.02), math.log(0.3))), 0.02, 0.3)
    vertical_table = jnp.clip(jnp.exp(math.log(1.0) - 2.3025851 * jax.random.uniform(arg_keys[9], (NCLASS, LEV), jnp.float32) ** shard_levels(arg_keys[9], (NCLASS, LEV), ((1, 4),), -0.2, 0.2)), 0.1, 1.0)
    return {"state": state, "eastward_current": eastward_current, "northward_current": northward_current, "obs_col": obs_col, "obs_row": obs_row, "obs_field": obs_field, "obs_class": obs_class, "obs_value": obs_value, "obs_error": obs_error, "vertical_table": vertical_table}


KAPPA_COEF = 0.2
EPSILON = 1e-05

def march_forward(field, eastward_current, northward_current):
    padded = jnp.pad(field, ((0, 0), (0, 0), (0, 0), (1, 1), (1, 1)))
    eastern = padded[:, :, :, 2:, 1:-1]
    western = padded[:, :, :, :-2, 1:-1]
    northern = padded[:, :, :, 1:-1, 2:]
    southern = padded[:, :, :, 1:-1, :-2]
    zonal = eastward_current[:, None, :]
    meridional = northward_current[:, None, :]
    tendency = -0.5 * zonal * (eastern - western) - 0.5 * meridional * (northern - southern) + KAPPA_COEF * (eastern + western + northern + southern - 4.0 * field)
    return field + tendency

def taper_weight(first_col, first_row, second_col, second_row, radius_col, radius_row):
    offset_col = (second_col - first_col).astype(jnp.float32) / radius_col
    offset_row = (second_row - first_row).astype(jnp.float32) / radius_row
    radial = 1.0 - offset_col * offset_col - offset_row * offset_row
    clipped = jnp.maximum(radial, 0.0)
    return clipped * clipped

def analysis_rows(priors, obs_value, obs_error):
    members = priors.shape[1]
    average = lax.optimization_barrier(jnp.mean(priors, axis=1, keepdims=True))
    spread = priors - average
    variance = lax.optimization_barrier(jnp.sum(spread * spread, axis=1, keepdims=True)) / (members - 1) + EPSILON
    error_var = obs_error[:, None]
    shrink = variance / (variance + error_var)
    factor = jnp.sqrt(error_var / (variance + error_var))
    increments = shrink * (obs_value[:, None] - average) + (factor - 1.0) * spread
    regress = spread / ((members - 1) * variance)
    return (increments, regress)

def reference(state, eastward_current, northward_current, obs_col, obs_row, obs_field, obs_class, obs_value, obs_error, vertical_table):
    field = state
    for predict_one_step in range(2):
        field = march_forward(field, eastward_current, northward_current)
    grid_cols = jnp.arange(NX, dtype=jnp.int32)
    grid_rows = jnp.arange(NY, dtype=jnp.int32)
    class_axis = jnp.arange(NCLASS, dtype=jnp.int32)
    for which_batch in range(NBATCH):
        column_ids = obs_col[which_batch]
        row_ids = obs_row[which_batch]
        field_ids = obs_field[which_batch]
        class_ids = obs_class[which_batch]
        picked = field[:, field_ids, :, column_ids, row_ids]
        priors = lax.optimization_barrier(jnp.sum(picked, axis=2)) / LEV
        increments, regress = analysis_rows(priors, obs_value[which_batch], obs_error[which_batch])
        horizontal = taper_weight(column_ids[:, None, None], row_ids[:, None, None], grid_cols[None, :, None], grid_rows[None, None, :], float(RADX), float(RADY))
        selector = (class_ids[:, None] == class_axis[None, :]).astype(jnp.float32)
        vertical = jnp.dot(selector, vertical_table, precision=lax.Precision.HIGHEST, preferred_element_type=jnp.float32)
        weights = vertical[:, :, None, None] * horizontal[:, None, :, :]
        updated = []
        for which_field in range(FIELDS):
            field_layer = field[:, which_field]
            anomaly = field_layer - lax.optimization_barrier(jnp.mean(field_layer, axis=0, keepdims=True))
            covariance = jnp.einsum('jm,mlxy->jlxy', regress, anomaly, precision=lax.Precision.HIGHEST)
            weighted = covariance * weights
            increment_field = jnp.einsum('jm,jlxy->mlxy', increments, weighted, precision=lax.Precision.HIGHEST)
            updated.append(field_layer + increment_field)
        field = jnp.stack(updated, axis=1)
    return field
```

```python
import jax
import jax.numpy as jnp
from jax import lax
from jax.experimental import pallas as pl
from jax.experimental.pallas import tpu as pltpu
from jax.sharding import Mesh, PartitionSpec as P

RADY = 40
KAPPA_COEF = 0.2
EPSILON = 1e-05
LANES = 128
TILES = ("z", "y", "core")


def forecast_kernel(
    place, present, state, left, right, east, north, meta, table, grid, mine, other, wide, sems
):
    members, fields, levels, columns, rows = state.shape
    halo = left.shape[3]
    batches = meta.shape[0]
    span = columns + 2 * halo
    groups = fields * levels
    first, core, origin = place[0], place[1], place[2]
    copies = []
    for f in range(fields):
        for l in range(levels):
            for k in range(span):
                if k < halo:
                    source = left.at[:, f, l, k, :]
                elif k < halo + columns:
                    source = state.at[:, f, l, k - halo, :]
                else:
                    source = right.at[:, f, l, k - halo - columns, :]
                slot = (f * levels + l) * span + k
                copies.append(pltpu.make_async_copy(source, wide.at[slot], sems.at[slot]))
    for copy in copies:
        copy.start()
    lane = lax.broadcasted_iota(jnp.int32, (1, rows), 1)
    for g in range(groups):
        for k in range(span):
            copies[g * span + k].wait()
        l = g % levels
        zonal = 0.5 * east[l : l + 1, :]
        meridional = 0.5 * north[l : l + 1, :]
        to_east = KAPPA_COEF - zonal
        to_west = KAPPA_COEF + zonal
        to_north = jnp.where(lane == rows - 1, 0.0, KAPPA_COEF - meridional)
        to_south = jnp.where(lane == 0, 0.0, KAPPA_COEF + meridional)

        def step(west, here, east_):
            north_ = pltpu.roll(here, rows - 1, 1)
            south_ = pltpu.roll(here, 1, 1)
            return (
                (1.0 - 4.0 * KAPPA_COEF) * here
                + to_east * east_
                + to_west * west
                + to_north * north_
                + to_south * south_
            )

        base = g * span
        once = []
        for k in range(1, span - 1):
            value = step(wide[base + k - 1], wide[base + k], wide[base + k + 1])
            if k < halo or k >= halo + columns:
                col = first + (k - halo)
                inside = jnp.logical_and(col >= 0, col < place[3])
                value = jnp.where(inside, value, 0.0)
            once.append(value)
        for k in range(columns):
            at = k + halo - 1
            grid[g * columns + k] = step(once[at - 1], once[at], once[at + 1])
    for out in (mine, other):
        out[batches * members :, :] = jnp.zeros(
            (out.shape[0] - batches * members, LANES), jnp.float32
        )
    vt = jnp.zeros((8, LANES), jnp.float32)
    spot = lax.broadcasted_iota(jnp.int32, (8, LANES), 1)
    for k in range(table.shape[0]):
        own_weight = jnp.where(core == 0, table[k, 0], table[k, 1])
        vt = jnp.where(spot == k, own_weight, vt)
    mine[batches * members : batches * members + 8, :] = jnp.where(origin == 1, vt, 0.0)

    def pick(b, carry):
        rows_of = pl.ds(pl.multiple_of(b * members, 8), members)

        @pl.when(present[b] == 0)
        def _():
            mine[rows_of, :] = jnp.zeros((members, LANES), jnp.float32)
            other[rows_of, :] = jnp.zeros((members, LANES), jnp.float32)

        @pl.when(present[b] != 0)
        def _():
            info = meta[b]
            target = info[2:3] * columns + (info[0:1] - first)
            inside = jnp.logical_and(info[0:1] >= first, info[0:1] < first + columns)
            target = jnp.where(inside, target, -1)
            target = jnp.broadcast_to(target, (members, LANES))
            index = jnp.broadcast_to(info[1:2], (members, LANES))
            for out, level in ((mine, core), (other, 1 - core)):
                total = jnp.zeros((members, LANES), jnp.float32)
                for f in range(fields):
                    for k in range(columns):
                        slab = grid[(f * levels + level) * columns + k]
                        picked = jnp.take_along_axis(slab, index, axis=1)
                        total = jnp.where(target == f * columns + k, picked, total)
                out[rows_of, :] = total

        return carry

    lax.fori_loop(0, batches, pick, 0)


def halves(x):
    high = x.astype(jnp.bfloat16)
    low = (x - high.astype(jnp.float32)).astype(jnp.bfloat16)
    return high, low


def analysis_kernel(
    place, table, info, near, far, grid, out, local, remote, spread_rows, spread_cols, vertical, profile, sems
):
    parts, length, _ = near.shape
    slabs, members, rows = grid.shape
    fields, levels, columns = out.shape[1], out.shape[2], out.shape[3]
    batches = info.shape[0]
    all_levels = 2 * parts
    total_cols = place[1].astype(jnp.float32)
    classes = table.shape[0]
    first = place[0].astype(jnp.float32)
    incoming = [
        pltpu.make_async_copy(near, remote.at[0:parts], sems.at[0]),
        pltpu.make_async_copy(far, remote.at[parts:all_levels], sems.at[1]),
        pltpu.make_async_copy(grid, local, sems.at[2]),
    ]
    for copy in incoming:
        copy.start()
    for copy in incoming:
        copy.wait()
    inverse = 1.0 / total_cols

    def update(x, weight):
        high, low = halves(x)
        covariance = jnp.dot(
            spread_cols[...],
            jnp.concatenate([high, high, low], axis=0),
            preferred_element_type=jnp.float32,
        )
        high, low = halves(covariance * weight)
        return x + jnp.dot(
            spread_rows[...],
            jnp.concatenate([high, high, low], axis=0),
            preferred_element_type=jnp.float32,
        )

    def batch(b, carry):
        mine = pl.ds(pl.multiple_of(b * members, 8), members)
        facts = info[b]
        priors = remote[0, mine, :]
        for level in range(1, all_levels):
            priors = priors + remote[level, mine, :]
        priors = priors * (1.0 / all_levels)
        average = jnp.sum(priors, axis=0, keepdims=True) * (1.0 / members)
        spread = priors - average
        variance = jnp.sum(spread * spread, axis=0, keepdims=True) / (members - 1) + EPSILON
        error = facts[4:5]
        ratio = 1.0 / (variance + error)
        shrink = variance * ratio
        factor = jnp.sqrt(error * ratio)
        increments = shrink * (facts[3:4] - average) + (factor - 1.0) * spread
        regress = spread / ((members - 1) * variance)
        high, low = halves(increments)
        spread_rows[...] = jnp.concatenate([high, low, high], axis=1)
        high = regress.astype(jnp.bfloat16).astype(jnp.float32)
        low = regress - high
        stacked = jnp.concatenate(
            [high, low, high, jnp.zeros((256 - 3 * members, LANES), jnp.float32)], axis=0
        )
        spread_cols[...] = jnp.transpose(stacked)[:, : 3 * members].astype(jnp.bfloat16)

        def column_of(k):
            return jnp.transpose(jnp.broadcast_to(facts[k : k + 1], (LANES, LANES)))

        obs_col, obs_row, obs_class = column_of(0), column_of(1), column_of(2)
        for level in range(all_levels + levels):
            if level < all_levels:
                row = remote[level, batches * members : batches * members + 8, :]
                weights = [
                    jnp.broadcast_to(row[0:1, k : k + 1], (LANES, LANES)) for k in range(classes)
                ]
            else:
                weights = [table[k, level - all_levels] for k in range(classes)]
            chosen = jnp.zeros((LANES, LANES), jnp.float32) + weights[classes - 1]
            for k in range(classes - 1):
                chosen = jnp.where(obs_class == float(k), weights[k], chosen)
            vertical[level] = chosen

        def later(c, carry):
            theirs = pl.ds(pl.multiple_of(c * members, 8), members)
            there = info[c]
            d_col = (there[0:1] - obs_col) * inverse
            d_row = (there[1:2] - obs_row) * (1.0 / RADY)
            radial = jnp.maximum(1.0 - d_col * d_col - d_row * d_row, 0.0)
            taper = radial * radial
            for level in range(0, all_levels, 2):
                x = jnp.concatenate([remote[level, theirs, :], remote[level + 1, theirs, :]], axis=1)
                weight = jnp.concatenate(
                    [taper * vertical[level], taper * vertical[level + 1]], axis=1
                )
                x = update(x, weight)
                remote[level, theirs, :] = x[:, :LANES]
                remote[level + 1, theirs, :] = x[:, LANES:]
            return carry

        lax.fori_loop(b + 1, batches, later, 0)
        lane = lax.broadcasted_iota(jnp.int32, (1, LANES), 1).astype(jnp.float32)
        d_row = (lane - obs_row) * (1.0 / RADY)
        profile[0] = 1.0 - d_row * d_row
        profile[1] = (first - obs_col) * inverse

        def cells(pair, carry):
            tapers = []
            for k in range(2):
                col = (2 * pair + k).astype(jnp.float32)
                d_col = profile[1] + col * inverse
                radial = jnp.maximum(profile[0] - d_col * d_col, 0.0)
                tapers.append(radial * radial)
            for level in range(levels):
                v = vertical[all_levels + level]
                weight = jnp.concatenate([tapers[0] * v, tapers[1] * v], axis=1)
                for f in range(fields):
                    at = (f * levels + level) * columns + 2 * pair
                    x = jnp.concatenate([local[at], local[at + 1]], axis=1)
                    x = update(x, weight)
                    local[at] = x[:, :LANES]
                    local[at + 1] = x[:, LANES:]
            return carry

        lax.fori_loop(0, columns // 2, cells, 0)
        return carry

    lax.fori_loop(0, batches, batch, 0)
    outgoing = []
    for f in range(fields):
        for level in range(levels):
            for k in range(columns):
                at = (f * levels + level) * columns + k
                outgoing.append(
                    pltpu.make_async_copy(
                        local.at[at], out.at[:, f, level, k, :], sems.at[3 + at]
                    )
                )
    for copy in outgoing:
        copy.start()
    for copy in outgoing:
        copy.wait()


def forecast(place, present, state, left, right, east, north, meta, table, length):
    members, fields, levels, columns, rows = state.shape
    halo = left.shape[3]
    slots = fields * levels * (columns + 2 * halo)
    smem = pl.BlockSpec(memory_space=pltpu.SMEM)
    vmem = pl.BlockSpec(memory_space=pltpu.VMEM)
    anywhere = pl.BlockSpec(memory_space=pl.ANY)
    picks = jax.ShapeDtypeStruct((length, LANES), jnp.float32)
    return pl.pallas_call(
        forecast_kernel,
        out_shape=(
            jax.ShapeDtypeStruct((fields * levels * columns, members, rows), jnp.float32),
            picks,
            picks,
        ),
        in_specs=[smem, smem, anywhere, anywhere, anywhere, vmem, vmem, vmem, smem],
        out_specs=(vmem, vmem, vmem),
        scratch_shapes=[
            pltpu.VMEM((slots, members, rows), jnp.float32),
            pltpu.SemaphoreType.DMA((slots,)),
        ],
        compiler_params=pltpu.CompilerParams(vmem_limit_bytes=40 * 2**20),
    )(place, present, state, left, right, east, north, meta, table)


def assimilate(place, table, info, near, far, grid, shape):
    members, fields, levels, columns, rows = shape
    smem = pl.BlockSpec(memory_space=pltpu.SMEM)
    vmem = pl.BlockSpec(memory_space=pltpu.VMEM)
    anywhere = pl.BlockSpec(memory_space=pl.ANY)
    parts, length, _ = near.shape
    return pl.pallas_call(
        analysis_kernel,
        out_shape=jax.ShapeDtypeStruct(shape, jnp.float32),
        in_specs=[smem, smem, vmem, anywhere, anywhere, anywhere],
        out_specs=anywhere,
        scratch_shapes=[
            pltpu.VMEM(grid.shape, jnp.float32),
            pltpu.VMEM((2 * parts, length, LANES), jnp.float32),
            pltpu.VMEM((members, 3 * LANES), jnp.bfloat16),
            pltpu.VMEM((LANES, 3 * members), jnp.bfloat16),
            pltpu.VMEM((2 * parts + levels, LANES, LANES), jnp.float32),
            pltpu.VMEM((2, LANES, LANES), jnp.float32),
            pltpu.SemaphoreType.DMA((3 + grid.shape[0],)),
        ],
        compiler_params=pltpu.CompilerParams(vmem_limit_bytes=40 * 2**20),
    )(place, table, info, near, far, grid)


def shards(
    state,
    eastward_current,
    northward_current,
    obs_col,
    obs_row,
    obs_field,
    obs_class,
    obs_value,
    obs_error,
    vertical_table,
):
    members, fields, levels, columns, rows = state.shape
    batches, obs = obs_col.shape
    homes = lax.axis_size("z") * lax.axis_size("y")
    tiles = homes * lax.axis_size("core")
    tile = lax.axis_index(TILES)
    core = lax.axis_index("core")
    first = tile * columns
    chunk = -(-(batches * members + 8) // (8 * homes)) * 8
    length = chunk * homes

    up = [(i, i + 1) for i in range(tiles - 1)]
    down = [(j, i) for i, j in up]
    left = lax.ppermute(state[:, :, :, columns - 2 :, :], TILES, up)
    right = lax.ppermute(state[:, :, :, :2, :], TILES, down)

    zero = jnp.zeros_like(obs_col)
    meta = jnp.stack([obs_col, obs_row, obs_field, zero, zero, zero, zero, zero], axis=1)
    inside = jnp.logical_and(obs_col >= first, obs_col < first + columns)
    present = jnp.any(inside, axis=1).astype(jnp.int32)
    origin = (tile // 2 == 0).astype(jnp.int32)
    place = jnp.stack([first, core, origin, jnp.int32(tiles * columns)]).astype(jnp.int32)
    grid, mine, other = forecast(
        place, present, state, left, right, eastward_current, northward_current, meta,
        vertical_table, length,
    )

    swap = [(0, 1), (1, 0)]
    mine = mine + lax.ppermute(other, "core", swap)
    mine = lax.all_to_all(mine.reshape(homes, chunk, LANES), ("z", "y"), 0, 0, tiled=True)
    mine = jnp.sum(mine, axis=0)
    mine = lax.all_to_all(
        jnp.broadcast_to(mine[None], (homes, chunk, LANES)), ("z", "y"), 0, 0, tiled=True
    )
    mine = mine.reshape(length, LANES)
    near = lax.all_gather(mine, "x")
    far = lax.ppermute(near, "core", swap)

    as_float = [v.astype(jnp.float32) for v in (obs_col, obs_row, obs_class)]
    blank = jnp.zeros_like(obs_value)
    info = jnp.stack([*as_float, obs_value, obs_error, blank, blank, blank], axis=1)
    where = jnp.stack([first, jnp.int32(tiles * columns)]).astype(jnp.int32)
    return assimilate(where, vertical_table, info, near, far, grid, state.shape)


def solution(mesh):
    fine = Mesh(mesh.devices.reshape(8, 8, 2, 4), ("z", "y", "core", "x"))
    state = P(None, None, "x", TILES, None)
    placed = (
        state,
        P("x", None),
        P("x", None),
        P(),
        P(),
        P(),
        P(),
        P(),
        P(),
        P(None, "x"),
    )
    return jax.shard_map(shards, mesh=fine, in_specs=placed, out_specs=state, check_vma=False)
```

```python
import functools

import jax
import jax.numpy as jnp
from jax import lax
from jax.experimental import pallas as pl
from jax.experimental.pallas import tpu as pltpu
from jax.sharding import Mesh, PartitionSpec as P

RADY = 40
KAPPA_COEF = 0.2
EPSILON = 1e-05
LANES = 128
TILES = ("z", "y", "core")


def forecast_kernel(
    place, table, state, east, north, cols, rws, flds, grid, to_left, to_right, mine, other,
    plain, ahead, seen, sems
):
    members, fields, levels, columns, rows = state.shape
    reach = 2
    batches = cols.shape[0]
    span = columns + 2 * reach
    groups = fields * levels
    first, core, origin, total_cols = place[0], place[1], place[2], place[3]
    copies = []
    for g in range(groups):
        for k in range(columns):
            slot = g * columns + k
            copies.append(
                pltpu.make_async_copy(
                    state.at[:, g // levels, g % levels, k, :], plain.at[slot], sems.at[slot]
                )
            )
    for copy in copies:
        copy.start()
    slot = cols[...] - (first - reach)
    near = jnp.where(jnp.logical_and(slot >= 0, slot < span), 1.0, 0.0)
    near = jnp.max(near, axis=1, keepdims=True)
    for b in range(batches):
        seen[b] = near[b, 0].astype(jnp.int32)
    lane = lax.broadcasted_iota(jnp.int32, (1, rows), 1)
    for g in range(groups):
        for k in range(columns):
            copies[g * columns + k].wait()
        l = g % levels
        zonal = 0.5 * east[l : l + 1, :]
        meridional = 0.5 * north[l : l + 1, :]
        to_east = KAPPA_COEF - zonal
        to_west = KAPPA_COEF + zonal
        to_north = jnp.where(lane == rows - 1, 0.0, KAPPA_COEF - meridional)
        to_south = jnp.where(lane == 0, 0.0, KAPPA_COEF + meridional)

        def step(west, here, east_):
            total = None
            if here is not None:
                total = (
                    (1.0 - 4.0 * KAPPA_COEF) * here
                    + to_north * pltpu.roll(here, rows - 1, 1)
                    + to_south * pltpu.roll(here, 1, 1)
                )
            if east_ is not None:
                total = to_east * east_ if total is None else total + to_east * east_
            if west is not None:
                total = to_west * west if total is None else total + to_west * west
            return total

        none = [None] * reach
        start = none + [plain[g * columns + k] for k in range(columns)] + none
        once = [None] * span
        for k in range(1, span - 1):
            value = step(start[k - 1], start[k], start[k + 1])
            if k < reach or k >= reach + columns:
                col = first + (k - reach)
                inside = jnp.logical_and(col >= 0, col < total_cols)
                value = jnp.where(inside, value, 0.0)
            once[k] = value
        for k in range(span):
            west = once[k - 1] if k > 0 else None
            east_ = once[k + 1] if k < span - 1 else None
            value = step(west, once[k], east_)
            ahead[g * span + k] = value
            if k < reach:
                to_left[g * reach + k] = value
            elif k < reach + columns:
                grid[g * columns + k - reach] = value
            else:
                to_right[g * reach + k - reach - columns] = value
    for out in (mine, other):
        out[batches * members :, :] = jnp.zeros(
            (out.shape[0] - batches * members, LANES), jnp.float32
        )
    vt = jnp.zeros((8, LANES), jnp.float32)
    spot = lax.broadcasted_iota(jnp.int32, (8, LANES), 1)
    for k in range(table.shape[0]):
        own_weight = jnp.where(core == 0, table[k, 0], table[k, 1])
        vt = jnp.where(spot == k, own_weight, vt)
    mine[batches * members : batches * members + 8, :] = jnp.where(origin == 1, vt, 0.0)

    def pick(b, carry):
        rows_of = pl.ds(pl.multiple_of(b * members, 8), members)
        slot = cols[pl.ds(b, 1), :] - (first - reach)
        inside = jnp.logical_and(slot >= 0, slot < span)
        target = jnp.where(inside, flds[pl.ds(b, 1), :] * span + slot, -1)
        present = seen[b] > 0

        @pl.when(jnp.logical_not(present))
        def _():
            mine[rows_of, :] = jnp.zeros((members, LANES), jnp.float32)
            other[rows_of, :] = jnp.zeros((members, LANES), jnp.float32)

        @pl.when(present)
        def _():
            wanted = jnp.broadcast_to(target, (members, LANES))
            index = jnp.broadcast_to(rws[pl.ds(b, 1), :], (members, LANES))
            for out, level in ((mine, core), (other, 1 - core)):
                total = jnp.zeros((members, LANES), jnp.float32)
                for f in range(fields):
                    for k in range(span):
                        slab = ahead[(f * levels + level) * span + k]
                        picked = jnp.take_along_axis(slab, index, axis=1)
                        total = jnp.where(wanted == f * span + k, picked, total)
                out[rows_of, :] = total

        return carry

    lax.fori_loop(0, batches, pick, 0)


def halves(x):
    high = x.astype(jnp.bfloat16)
    low = (x - high.astype(jnp.float32)).astype(jnp.bfloat16)
    return high, low


def analysis_kernel(count, place, table, info, *refs):
    arrived, rest = refs[:count], refs[count:]
    grid, from_left, from_right, out = rest[:4]
    local, remote, edges, spread_rows, spread_cols, vertical, sems = rest[4:]
    all_levels, length, _ = remote.shape
    slabs, members, rows = grid.shape
    fields, levels, columns = out.shape[1], out.shape[2], out.shape[3]
    groups = fields * levels
    batches = info.shape[0]
    total_cols = place[1].astype(jnp.float32)
    classes = table.shape[0]
    first = place[0].astype(jnp.float32)
    incoming = []
    level, at = 0, 0
    for ref in arrived:
        size = ref.shape[0]
        incoming.append((ref, remote.at[level, at : at + size]))
        at += size
        if at == length:
            level, at = level + 1, 0
    incoming += [(grid, local), (from_left, edges.at[0]), (from_right, edges.at[1])]
    incoming = [
        pltpu.make_async_copy(ref, target, sems.at[slabs + n])
        for n, (ref, target) in enumerate(incoming)
    ]
    for copy in incoming:
        copy.start()
    for copy in incoming:
        copy.wait()
    for g in range(groups):
        for k in range(2):
            west, east = g * columns + k, g * columns + columns - 2 + k
            local[west] = local[west] + edges[0, g * 2 + k]
            local[east] = local[east] + edges[1, g * 2 + k]
    inverse = 1.0 / total_cols

    def update(x, weight):
        high, low = halves(x)
        covariance = jnp.dot(
            spread_cols[...],
            jnp.concatenate([high, high, low], axis=0),
            preferred_element_type=jnp.float32,
        )
        change = jnp.dot(
            spread_rows[...],
            jnp.concatenate(halves(covariance * weight), axis=0),
            preferred_element_type=jnp.float32,
        )
        return x + (change[:members] + change[members:])

    def batch(b, carry):
        mine = pl.ds(pl.multiple_of(b * members, 8), members)
        facts = info[b]
        priors = remote[0, mine, :]
        for level in range(1, all_levels):
            priors = priors + remote[level, mine, :]
        priors = priors * (1.0 / all_levels)
        average = jnp.sum(priors, axis=0, keepdims=True) * (1.0 / members)
        spread = priors - average
        variance = jnp.sum(spread * spread, axis=0, keepdims=True) / (members - 1) + EPSILON
        error = facts[4:5]
        ratio = 1.0 / (variance + error)
        shrink = variance * ratio
        factor = jnp.sqrt(error * ratio)
        increments = shrink * (facts[3:4] - average) + (factor - 1.0) * spread
        regress = spread / ((members - 1) * variance)
        high, low = halves(increments)
        spread_rows[:members, :LANES] = high
        spread_rows[:members, LANES:] = high
        spread_rows[members:, :LANES] = low
        spread_rows[members:, LANES:] = jnp.zeros_like(low)
        high = regress.astype(jnp.bfloat16).astype(jnp.float32)
        low = regress - high
        stacked = jnp.concatenate(
            [high, low, high, jnp.zeros((256 - 3 * members, LANES), jnp.float32)], axis=0
        )
        spread_cols[...] = jnp.transpose(stacked)[:, : 3 * members].astype(jnp.bfloat16)

        def column_of(k):
            return jnp.transpose(jnp.broadcast_to(facts[k : k + 1], (LANES, LANES)))

        obs_col, obs_row, obs_class = column_of(0), column_of(1), column_of(2)
        for level in range(all_levels + levels):
            if level < all_levels:
                row = remote[level, batches * members : batches * members + 8, :]
                weights = [
                    jnp.broadcast_to(row[0:1, k : k + 1], (LANES, LANES)) for k in range(classes)
                ]
            else:
                weights = [table[k, level - all_levels] for k in range(classes)]
            chosen = jnp.zeros((LANES, LANES), jnp.float32) + weights[classes - 1]
            for k in range(classes - 1):
                chosen = jnp.where(obs_class == float(k), weights[k], chosen)
            vertical[level] = chosen

        def later_many(c0, many):
            xs, ws, keep = [], [], []
            for k in range(many):
                c = c0 + k
                theirs = pl.ds(pl.multiple_of(c * members, 8), members)
                there = info[c]
                d_col = (there[0:1] - obs_col) * inverse
                d_row = (there[1:2] - obs_row) * (1.0 / RADY)
                radial = jnp.maximum(1.0 - d_col * d_col - d_row * d_row, 0.0)
                taper = radial * radial
                for g in range(all_levels):
                    xs.append(remote[g, theirs, :])
                    ws.append(taper * vertical[g])
                    keep.append((g, theirs))
            x = update(jnp.concatenate(xs, axis=1), jnp.concatenate(ws, axis=1))
            for n, (g, theirs) in enumerate(keep):
                remote[g, theirs, :] = x[:, n * LANES : (n + 1) * LANES]

        count = batches - 1 - b

        for size in (1, 2):

            @pl.when((count // size) % 2 == 1)
            def _():
                later_many(b + 1 + (count % size), size)

        start = b + 1 + count % 4

        def four(i, carry):
            later_many(start + 4 * i, 4)
            return carry

        lax.fori_loop(0, count // 4, four, 0)
        lane = lax.broadcasted_iota(jnp.int32, (1, LANES), 1).astype(jnp.float32)
        d_row = (lane - obs_row) * (1.0 / RADY)
        across = 1.0 - d_row * d_row
        along = (first - obs_col) * inverse
        xs, ws = [], []
        for k in range(columns):
            d_col = along + k * inverse
            radial = jnp.maximum(across - d_col * d_col, 0.0)
            taper = radial * radial
            for level in range(levels):
                weight = taper * vertical[all_levels + level]
                for f in range(fields):
                    xs.append((f * levels + level) * columns + k)
                    ws.append(weight)
        step = 24
        for n in range(0, len(xs), step):
            x = update(
                jnp.concatenate([local[at] for at in xs[n : n + step]], axis=1),
                jnp.concatenate(ws[n : n + step], axis=1),
            )
            for i, at in enumerate(xs[n : n + step]):
                local[at] = x[:, i * LANES : (i + 1) * LANES]
        return carry

    lax.fori_loop(0, batches, batch, 0)
    outgoing = []
    for f in range(fields):
        for level in range(levels):
            for k in range(columns):
                at = (f * levels + level) * columns + k
                outgoing.append(
                    pltpu.make_async_copy(
                        local.at[at], out.at[:, f, level, k, :], sems.at[at]
                    )
                )
    for copy in outgoing:
        copy.start()
    for copy in outgoing:
        copy.wait()


def forecast(place, table, state, east, north, cols, rws, flds, length):
    members, fields, levels, columns, rows = state.shape
    groups = fields * levels
    smem = pl.BlockSpec(memory_space=pltpu.SMEM)
    vmem = pl.BlockSpec(memory_space=pltpu.VMEM)
    anywhere = pl.BlockSpec(memory_space=pl.ANY)
    picks = jax.ShapeDtypeStruct((length, LANES), jnp.float32)
    edge = jax.ShapeDtypeStruct((groups * 2, members, rows), jnp.float32)
    return pl.pallas_call(
        forecast_kernel,
        out_shape=(
            jax.ShapeDtypeStruct((groups * columns, members, rows), jnp.float32),
            edge,
            edge,
            picks,
            picks,
        ),
        in_specs=[smem, smem, anywhere] + [vmem] * 5,
        out_specs=(vmem,) * 5,
        scratch_shapes=[
            pltpu.VMEM((groups * columns, members, rows), jnp.float32),
            pltpu.VMEM((groups * (columns + 4), members, rows), jnp.float32),
            pltpu.SMEM((cols.shape[0],), jnp.int32),
            pltpu.SemaphoreType.DMA((groups * columns,)),
        ],
        compiler_params=pltpu.CompilerParams(vmem_limit_bytes=40 * 2**20),
    )(place, table, state, east, north, cols, rws, flds)


def assimilate(place, table, info, arrived, grid, from_left, from_right, shape, length):
    members, fields, levels, columns, rows = shape
    smem = pl.BlockSpec(memory_space=pltpu.SMEM)
    vmem = pl.BlockSpec(memory_space=pltpu.VMEM)
    anywhere = pl.BlockSpec(memory_space=pl.ANY)
    all_levels = sum(part.shape[0] for part in arrived) // length
    return pl.pallas_call(
        functools.partial(analysis_kernel, len(arrived)),
        out_shape=jax.ShapeDtypeStruct(shape, jnp.float32),
        in_specs=[smem, smem, vmem] + [anywhere] * (len(arrived) + 3),
        out_specs=anywhere,
        scratch_shapes=[
            pltpu.VMEM(grid.shape, jnp.float32),
            pltpu.VMEM((all_levels, length, LANES), jnp.float32),
            pltpu.VMEM((2,) + from_left.shape, jnp.float32),
            pltpu.VMEM((2 * members, 2 * LANES), jnp.bfloat16),
            pltpu.VMEM((LANES, 3 * members), jnp.bfloat16),
            pltpu.VMEM((all_levels + levels, LANES, LANES), jnp.float32),
            pltpu.SemaphoreType.DMA((grid.shape[0] + len(arrived) + 3,)),
        ],
        compiler_params=pltpu.CompilerParams(vmem_limit_bytes=48 * 2**20),
    )(place, table, info, *arrived, grid, from_left, from_right)


def shards(
    state,
    eastward_current,
    northward_current,
    obs_col,
    obs_row,
    obs_field,
    obs_class,
    obs_value,
    obs_error,
    vertical_table,
):
    members, fields, levels, columns, rows = state.shape
    batches, obs = obs_col.shape
    homes = lax.axis_size("z") * lax.axis_size("y")
    tiles = homes * lax.axis_size("core")
    tile = lax.axis_index(TILES)
    core = lax.axis_index("core")
    first = tile * columns
    chunk = -(-(batches * members + 8) // (8 * homes)) * 8
    length = chunk * homes

    origin = (tile // 2 == 0).astype(jnp.int32)
    place = jnp.stack([first, core, origin, jnp.int32(tiles * columns)]).astype(jnp.int32)
    grid, to_left, to_right, mine, other = forecast(
        place, vertical_table, state, eastward_current, northward_current, obs_col, obs_row,
        obs_field, length,
    )

    swap = [(0, 1), (1, 0)]
    mine = mine + lax.ppermute(other, "core", swap)
    mine = lax.all_to_all(mine.reshape(homes, chunk, LANES), ("z", "y"), 0, 0, tiled=True)
    mine = jnp.sum(mine, axis=0)
    mine = lax.all_to_all(
        jnp.broadcast_to(mine[None], (homes, chunk, LANES)), ("z", "y"), 0, 0, tiled=True
    )
    mine = mine.reshape(length, LANES)

    mine, to_left, to_right = lax.optimization_barrier((mine, to_left, to_right))
    ring = lax.axis_size("x")
    right = [(i, (i + 1) % ring) for i in range(ring)]
    left = [(j, i) for i, j in right]
    before = lax.ppermute(mine, "x", right)
    after = lax.ppermute(mine, "x", left)
    across_a = lax.ppermute(after[: length // 2], "x", left)
    across_b = lax.ppermute(before[length // 2 :], "x", right)
    parts = [mine, before, after, across_a, across_b]
    arrived = parts + [lax.ppermute(part, "core", swap) for part in parts]
    up = [(i, i + 1) for i in range(tiles - 1)]
    down = [(j, i) for i, j in up]
    from_left = lax.ppermute(to_right, TILES, up)
    from_right = lax.ppermute(to_left, TILES, down)

    as_float = [v.astype(jnp.float32) for v in (obs_col, obs_row, obs_class)]
    blank = jnp.zeros_like(obs_value)
    info = jnp.stack([*as_float, obs_value, obs_error, blank, blank, blank], axis=1)
    where = jnp.stack([first, jnp.int32(tiles * columns)]).astype(jnp.int32)
    return assimilate(
        where, vertical_table, info, arrived, grid, from_left, from_right, state.shape, length
    )


def solution(mesh):
    fine = Mesh(mesh.devices.reshape(8, 8, 2, 4), ("z", "y", "core", "x"))
    state = P(None, None, "x", TILES, None)
    placed = (
        state,
        P("x", None),
        P("x", None),
        P(),
        P(),
        P(),
        P(),
        P(),
        P(),
        P(None, "x"),
    )
    return jax.shard_map(shards, mesh=fine, in_specs=placed, out_specs=state, check_vma=False)
```

```python
import functools

import jax
import jax.numpy as jnp
from jax import lax
from jax.experimental import pallas as pl
from jax.experimental.pallas import tpu as pltpu
from jax.sharding import Mesh, PartitionSpec as P

RADY = 40
KAPPA_COEF = 0.2
EPSILON = 1e-05
LANES = 128
TILES = ("z", "y", "core")


def forecast_kernel(
    place, table, state, east, north, cols, rws, flds, grid, to_left, to_right, mine, other,
    plain, ahead, seen, sems
):
    members, fields, levels, columns, rows = state.shape
    reach = 2
    batches = cols.shape[0]
    span = columns + 2 * reach
    groups = fields * levels
    first, core, origin, total_cols = place[0], place[1], place[2], place[3]
    copies = []
    for g in range(groups):
        for k in range(columns):
            slot = g * columns + k
            copies.append(
                pltpu.make_async_copy(
                    state.at[:, g // levels, g % levels, k, :], plain.at[slot], sems.at[slot]
                )
            )
    for copy in copies:
        copy.start()
    slot = cols[...] - (first - reach)
    near = jnp.where(jnp.logical_and(slot >= 0, slot < span), 1.0, 0.0)
    near = jnp.max(near, axis=1, keepdims=True)
    for b in range(batches):
        seen[b] = near[b, 0].astype(jnp.int32)
    lane = lax.broadcasted_iota(jnp.int32, (1, rows), 1)
    for g in range(groups):
        for k in range(columns):
            copies[g * columns + k].wait()
        l = g % levels
        zonal = 0.5 * east[l : l + 1, :]
        meridional = 0.5 * north[l : l + 1, :]
        to_east = KAPPA_COEF - zonal
        to_west = KAPPA_COEF + zonal
        to_north = jnp.where(lane == rows - 1, 0.0, KAPPA_COEF - meridional)
        to_south = jnp.where(lane == 0, 0.0, KAPPA_COEF + meridional)

        def step(west, here, east_):
            total = None
            if here is not None:
                total = (
                    (1.0 - 4.0 * KAPPA_COEF) * here
                    + to_north * pltpu.roll(here, rows - 1, 1)
                    + to_south * pltpu.roll(here, 1, 1)
                )
            if east_ is not None:
                total = to_east * east_ if total is None else total + to_east * east_
            if west is not None:
                total = to_west * west if total is None else total + to_west * west
            return total

        none = [None] * reach
        start = none + [plain[g * columns + k] for k in range(columns)] + none
        once = [None] * span
        for k in range(1, span - 1):
            value = step(start[k - 1], start[k], start[k + 1])
            if k < reach or k >= reach + columns:
                col = first + (k - reach)
                inside = jnp.logical_and(col >= 0, col < total_cols)
                value = jnp.where(inside, value, 0.0)
            once[k] = value
        for k in range(span):
            west = once[k - 1] if k > 0 else None
            east_ = once[k + 1] if k < span - 1 else None
            value = step(west, once[k], east_)
            ahead[g * span + k] = value
            if k < reach:
                to_left[g * reach + k] = value
            elif k < reach + columns:
                grid[g * columns + k - reach] = value
            else:
                to_right[g * reach + k - reach - columns] = value
    for out in (mine, other):
        out[batches * members :, :] = jnp.zeros(
            (out.shape[0] - batches * members, LANES), jnp.float32
        )
    vt = jnp.zeros((8, LANES), jnp.float32)
    spot = lax.broadcasted_iota(jnp.int32, (8, LANES), 1)
    for k in range(table.shape[0]):
        own_weight = jnp.where(core == 0, table[k, 0], table[k, 1])
        vt = jnp.where(spot == k, own_weight, vt)
    mine[batches * members : batches * members + 8, :] = jnp.where(origin == 1, vt, 0.0)

    def pick(b, carry):
        rows_of = pl.ds(pl.multiple_of(b * members, 8), members)
        slot = cols[pl.ds(b, 1), :] - (first - reach)
        inside = jnp.logical_and(slot >= 0, slot < span)
        target = jnp.where(inside, flds[pl.ds(b, 1), :] * span + slot, -1)
        present = seen[b] > 0

        @pl.when(jnp.logical_not(present))
        def _():
            mine[rows_of, :] = jnp.zeros((members, LANES), jnp.float32)
            other[rows_of, :] = jnp.zeros((members, LANES), jnp.float32)

        @pl.when(present)
        def _():
            wanted = jnp.broadcast_to(target, (members, LANES))
            index = jnp.broadcast_to(rws[pl.ds(b, 1), :], (members, LANES))
            for out, level in ((mine, core), (other, 1 - core)):
                total = jnp.zeros((members, LANES), jnp.float32)
                for f in range(fields):
                    for k in range(span):
                        slab = ahead[(f * levels + level) * span + k]
                        picked = jnp.take_along_axis(slab, index, axis=1)
                        total = jnp.where(wanted == f * span + k, picked, total)
                out[rows_of, :] = total

        return carry

    lax.fori_loop(0, batches, pick, 0)


def halves(x):
    high = x.astype(jnp.bfloat16)
    low = (x - high.astype(jnp.float32)).astype(jnp.bfloat16)
    return high, low


def analysis_kernel(count, place, table, info, *refs):
    arrived, rest = refs[:count], refs[count:]
    grid, from_left, from_right, out = rest[:4]
    local, remote, edges, spread_rows, spread_cols, vertical, sems = rest[4:]
    all_levels, length, _ = remote.shape
    slabs, members, rows = grid.shape
    fields, levels, columns = out.shape[1], out.shape[2], out.shape[3]
    groups = fields * levels
    batches = info.shape[0]
    total_cols = place[1].astype(jnp.float32)
    classes = table.shape[0]
    first = place[0].astype(jnp.float32)
    incoming = []
    level, at = 0, 0
    for ref in arrived:
        size = ref.shape[0]
        incoming.append((ref, remote.at[level, at : at + size]))
        at += size
        if at == length:
            level, at = level + 1, 0
    incoming += [(grid, local), (from_left, edges.at[0]), (from_right, edges.at[1])]
    incoming = [
        pltpu.make_async_copy(ref, target, sems.at[slabs + n])
        for n, (ref, target) in enumerate(incoming)
    ]
    for copy in incoming:
        copy.start()
    for copy in incoming:
        copy.wait()
    for g in range(groups):
        for k in range(2):
            west, east = g * columns + k, g * columns + columns - 2 + k
            local[west] = local[west] + edges[0, g * 2 + k]
            local[east] = local[east] + edges[1, g * 2 + k]
    inverse = 1.0 / total_cols

    def update(x, weight):
        high, low = halves(x)
        covariance = jnp.dot(
            spread_cols[...],
            jnp.concatenate([high, high, low], axis=0),
            preferred_element_type=jnp.float32,
        )
        change = jnp.dot(
            spread_rows[...],
            jnp.concatenate(halves(covariance * weight), axis=0),
            preferred_element_type=jnp.float32,
        )
        return x + (change[:members] + change[members:])

    def batch(b, carry):
        mine = pl.ds(pl.multiple_of(b * members, 8), members)
        facts = info[b]
        priors = remote[0, mine, :]
        for level in range(1, all_levels):
            priors = priors + remote[level, mine, :]
        priors = priors * (1.0 / all_levels)
        average = jnp.sum(priors, axis=0, keepdims=True) * (1.0 / members)
        spread = priors - average
        variance = jnp.sum(spread * spread, axis=0, keepdims=True) / (members - 1) + EPSILON
        error = facts[4:5]
        ratio = 1.0 / (variance + error)
        shrink = variance * ratio
        factor = jnp.sqrt(error * ratio)
        increments = shrink * (facts[3:4] - average) + (factor - 1.0) * spread
        regress = spread / ((members - 1) * variance)
        high, low = halves(increments)
        spread_rows[:members, :LANES] = high
        spread_rows[:members, LANES:] = high
        spread_rows[members:, :LANES] = low
        spread_rows[members:, LANES:] = jnp.zeros_like(low)
        high = regress.astype(jnp.bfloat16).astype(jnp.float32)
        low = regress - high
        stacked = jnp.concatenate(
            [high, low, high, jnp.zeros((256 - 3 * members, LANES), jnp.float32)], axis=0
        )
        spread_cols[...] = jnp.transpose(stacked)[:, : 3 * members].astype(jnp.bfloat16)

        def column_of(k):
            return jnp.transpose(jnp.broadcast_to(facts[k : k + 1], (LANES, LANES)))

        obs_col, obs_row, obs_class = column_of(0), column_of(1), column_of(2)
        for level in range(all_levels + levels):
            if level < all_levels:
                row = remote[level, batches * members : batches * members + 8, :]
                weights = [
                    jnp.broadcast_to(row[0:1, k : k + 1], (LANES, LANES)) for k in range(classes)
                ]
            else:
                weights = [table[k, level - all_levels] for k in range(classes)]
            chosen = jnp.zeros((LANES, LANES), jnp.float32) + weights[classes - 1]
            for k in range(classes - 1):
                chosen = jnp.where(obs_class == float(k), weights[k], chosen)
            vertical[level] = chosen

        def later_many(c0, many):
            xs, ws, keep = [], [], []
            for k in range(many):
                c = c0 + k
                theirs = pl.ds(pl.multiple_of(c * members, 8), members)
                there = info[c]
                d_col = (there[0:1] - obs_col) * inverse
                d_row = (there[1:2] - obs_row) * (1.0 / RADY)
                radial = jnp.maximum(1.0 - d_col * d_col - d_row * d_row, 0.0)
                taper = radial * radial
                for g in range(all_levels):
                    xs.append(remote[g, theirs, :])
                    ws.append(taper * vertical[g])
                    keep.append((g, theirs))
            x = update(jnp.concatenate(xs, axis=1), jnp.concatenate(ws, axis=1))
            for n, (g, theirs) in enumerate(keep):
                remote[g, theirs, :] = x[:, n * LANES : (n + 1) * LANES]

        count = batches - 1 - b

        for size in (1, 2):

            @pl.when((count // size) % 2 == 1)
            def _():
                later_many(b + 1 + (count % size), size)

        start = b + 1 + count % 4

        def four(i, carry):
            later_many(start + 4 * i, 4)
            return carry

        lax.fori_loop(0, count // 4, four, 0)
        lane = lax.broadcasted_iota(jnp.int32, (1, LANES), 1).astype(jnp.float32)
        d_row = (lane - obs_row) * (1.0 / RADY)
        across = 1.0 - d_row * d_row
        along = (first - obs_col) * inverse
        xs, ws = [], []
        for k in range(columns):
            d_col = along + k * inverse
            radial = jnp.maximum(across - d_col * d_col, 0.0)
            taper = radial * radial
            for level in range(levels):
                weight = taper * vertical[all_levels + level]
                for f in range(fields):
                    xs.append((f * levels + level) * columns + k)
                    ws.append(weight)
        step = 24
        for n in range(0, len(xs), step):
            x = update(
                jnp.concatenate([local[at] for at in xs[n : n + step]], axis=1),
                jnp.concatenate(ws[n : n + step], axis=1),
            )
            for i, at in enumerate(xs[n : n + step]):
                local[at] = x[:, i * LANES : (i + 1) * LANES]
        return carry

    lax.fori_loop(0, batches, batch, 0)
    outgoing = []
    for f in range(fields):
        for level in range(levels):
            for k in range(columns):
                at = (f * levels + level) * columns + k
                outgoing.append(
                    pltpu.make_async_copy(
                        local.at[at], out.at[:, f, level, k, :], sems.at[at]
                    )
                )
    for copy in outgoing:
        copy.start()
    for copy in outgoing:
        copy.wait()


def forecast(place, table, state, east, north, cols, rws, flds, length):
    members, fields, levels, columns, rows = state.shape
    groups = fields * levels
    smem = pl.BlockSpec(memory_space=pltpu.SMEM)
    vmem = pl.BlockSpec(memory_space=pltpu.VMEM)
    anywhere = pl.BlockSpec(memory_space=pl.ANY)
    picks = jax.ShapeDtypeStruct((length, LANES), jnp.float32)
    edge = jax.ShapeDtypeStruct((groups * 2, members, rows), jnp.float32)
    return pl.pallas_call(
        forecast_kernel,
        out_shape=(
            jax.ShapeDtypeStruct((groups * columns, members, rows), jnp.float32),
            edge,
            edge,
            picks,
            picks,
        ),
        in_specs=[smem, smem, anywhere] + [vmem] * 5,
        out_specs=(vmem,) * 5,
        scratch_shapes=[
            pltpu.VMEM((groups * columns, members, rows), jnp.float32),
            pltpu.VMEM((groups * (columns + 4), members, rows), jnp.float32),
            pltpu.SMEM((cols.shape[0],), jnp.int32),
            pltpu.SemaphoreType.DMA((groups * columns,)),
        ],
        compiler_params=pltpu.CompilerParams(vmem_limit_bytes=16 * 2**20),
    )(place, table, state, east, north, cols, rws, flds)


def assimilate(place, table, info, arrived, grid, from_left, from_right, shape, length):
    members, fields, levels, columns, rows = shape
    smem = pl.BlockSpec(memory_space=pltpu.SMEM)
    vmem = pl.BlockSpec(memory_space=pltpu.VMEM)
    anywhere = pl.BlockSpec(memory_space=pl.ANY)
    all_levels = sum(part.shape[0] for part in arrived) // length
    return pl.pallas_call(
        functools.partial(analysis_kernel, len(arrived)),
        out_shape=jax.ShapeDtypeStruct(shape, jnp.float32),
        in_specs=[smem, smem, vmem] + [anywhere] * (len(arrived) + 3),
        out_specs=anywhere,
        scratch_shapes=[
            pltpu.VMEM(grid.shape, jnp.float32),
            pltpu.VMEM((all_levels, length, LANES), jnp.float32),
            pltpu.VMEM((2,) + from_left.shape, jnp.float32),
            pltpu.VMEM((2 * members, 2 * LANES), jnp.bfloat16),
            pltpu.VMEM((LANES, 3 * members), jnp.bfloat16),
            pltpu.VMEM((all_levels + levels, LANES, LANES), jnp.float32),
            pltpu.SemaphoreType.DMA((grid.shape[0] + len(arrived) + 3,)),
        ],
        compiler_params=pltpu.CompilerParams(vmem_limit_bytes=28 * 2**20),
    )(place, table, info, *arrived, grid, from_left, from_right)


def shards(
    state,
    eastward_current,
    northward_current,
    obs_col,
    obs_row,
    obs_field,
    obs_class,
    obs_value,
    obs_error,
    vertical_table,
):
    members, fields, levels, columns, rows = state.shape
    batches, obs = obs_col.shape
    homes = lax.axis_size("z") * lax.axis_size("y")
    tiles = homes * lax.axis_size("core")
    tile = lax.axis_index(TILES)
    core = lax.axis_index("core")
    first = tile * columns
    chunk = -(-(batches * members + 8) // (8 * homes)) * 8
    length = chunk * homes

    origin = (tile // 2 == 0).astype(jnp.int32)
    place = jnp.stack([first, core, origin, jnp.int32(tiles * columns)]).astype(jnp.int32)
    grid, to_left, to_right, mine, other = forecast(
        place, vertical_table, state, eastward_current, northward_current, obs_col, obs_row,
        obs_field, length,
    )

    swap = [(0, 1), (1, 0)]
    mine = mine + lax.ppermute(other, "core", swap)
    mine = lax.all_to_all(mine.reshape(homes, chunk, LANES), ("z", "y"), 0, 0, tiled=True)
    mine = jnp.sum(mine, axis=0)
    mine = lax.all_to_all(
        jnp.broadcast_to(mine[None], (homes, chunk, LANES)), ("z", "y"), 0, 0, tiled=True
    )
    mine = mine.reshape(length, LANES)

    ring = lax.axis_size("x")
    both_ways = [(i, (i + 1) % ring) for i in range(ring)]
    both_ways += [(ring + (i + 1) % ring, ring + i) for i in range(ring)]

    def ship(part):
        return lax.ppermute(part, ("core", "x"), both_ways)

    def other_core(part):
        return lax.ppermute(part, "core", swap)

    beside = ship(mine)
    mate = other_core(mine)
    mated = ship(mate)
    opposite = ship(beside)
    mated, to_left, to_right = lax.optimization_barrier((mated, to_left, to_right))
    arrived = [mine, mate, beside, mated, opposite]
    arrived += [other_core(part) for part in (beside, mated, opposite)]
    up = [(i, i + 1) for i in range(tiles - 1)]
    down = [(j, i) for i, j in up]
    from_left = lax.ppermute(to_right, TILES, up)
    from_right = lax.ppermute(to_left, TILES, down)

    as_float = [v.astype(jnp.float32) for v in (obs_col, obs_row, obs_class)]
    blank = jnp.zeros_like(obs_value)
    info = jnp.stack([*as_float, obs_value, obs_error, blank, blank, blank], axis=1)
    where = jnp.stack([first, jnp.int32(tiles * columns)]).astype(jnp.int32)
    return assimilate(
        where, vertical_table, info, arrived, grid, from_left, from_right, state.shape, length
    )


def solution(mesh):
    fine = Mesh(mesh.devices.reshape(8, 8, 2, 4), ("z", "y", "core", "x"))
    state = P(None, None, "x", TILES, None)
    placed = (
        state,
        P("x", None),
        P("x", None),
        P(),
        P(),
        P(),
        P(),
        P(),
        P(),
        P(None, "x"),
    )
    return jax.shard_map(shards, mesh=fine, in_specs=placed, out_specs=state, check_vma=False)
```

```python
import functools

import jax
import jax.numpy as jnp
from jax import lax
from jax.experimental import pallas as pl
from jax.experimental.pallas import tpu as pltpu
from jax.sharding import Mesh, PartitionSpec as P

RADY = 40
KAPPA_COEF = 0.2
EPSILON = 1e-05
LANES = 128
TILES = ("z", "y", "core")


def forecast_kernel(
    place, table, state, east, north, cols, rws, flds, grid, to_left, to_right, mine, other,
    plain, ahead, seen, sems
):
    members, fields, levels, columns, rows = state.shape
    reach = 2
    batches = cols.shape[0]
    span = columns + 2 * reach
    groups = fields * levels
    first, core, origin, total_cols = place[0], place[1], place[2], place[3]
    copies = []
    for g in range(groups):
        for k in range(columns):
            slot = g * columns + k
            copies.append(
                pltpu.make_async_copy(
                    state.at[:, g // levels, g % levels, k, :], plain.at[slot], sems.at[slot]
                )
            )
    for copy in copies:
        copy.start()
    slot = cols[...] - (first - reach)
    near = jnp.where(jnp.logical_and(slot >= 0, slot < span), 1.0, 0.0)
    near = jnp.max(near, axis=1, keepdims=True)
    for b in range(batches):
        seen[b] = near[b, 0].astype(jnp.int32)
    lane = lax.broadcasted_iota(jnp.int32, (1, rows), 1)
    for g in range(groups):
        for k in range(columns):
            copies[g * columns + k].wait()
        l = g % levels
        zonal = 0.5 * east[l : l + 1, :]
        meridional = 0.5 * north[l : l + 1, :]
        to_east = KAPPA_COEF - zonal
        to_west = KAPPA_COEF + zonal
        to_north = jnp.where(lane == rows - 1, 0.0, KAPPA_COEF - meridional)
        to_south = jnp.where(lane == 0, 0.0, KAPPA_COEF + meridional)

        def step(west, here, east_):
            total = None
            if here is not None:
                total = (
                    (1.0 - 4.0 * KAPPA_COEF) * here
                    + to_north * pltpu.roll(here, rows - 1, 1)
                    + to_south * pltpu.roll(here, 1, 1)
                )
            if east_ is not None:
                total = to_east * east_ if total is None else total + to_east * east_
            if west is not None:
                total = to_west * west if total is None else total + to_west * west
            return total

        none = [None] * reach
        start = none + [plain[g * columns + k] for k in range(columns)] + none
        once = [None] * span
        for k in range(1, span - 1):
            value = step(start[k - 1], start[k], start[k + 1])
            if k < reach or k >= reach + columns:
                col = first + (k - reach)
                inside = jnp.logical_and(col >= 0, col < total_cols)
                value = jnp.where(inside, value, 0.0)
            once[k] = value
        for k in range(span):
            west = once[k - 1] if k > 0 else None
            east_ = once[k + 1] if k < span - 1 else None
            value = step(west, once[k], east_)
            ahead[g * span + k] = value
            if k < reach:
                to_left[g * reach + k] = value
            elif k < reach + columns:
                grid[g * columns + k - reach] = value
            else:
                to_right[g * reach + k - reach - columns] = value
    for out in (mine, other):
        out[batches * members :, :] = jnp.zeros(
            (out.shape[0] - batches * members, LANES), jnp.float32
        )
    vt = jnp.zeros((8, LANES), jnp.float32)
    spot = lax.broadcasted_iota(jnp.int32, (8, LANES), 1)
    for k in range(table.shape[0]):
        own_weight = jnp.where(core == 0, table[k, 0], table[k, 1])
        vt = jnp.where(spot == k, own_weight, vt)
    mine[batches * members : batches * members + 8, :] = jnp.where(origin == 1, vt, 0.0)

    def pick(b, carry):
        rows_of = pl.ds(pl.multiple_of(b * members, 8), members)
        slot = cols[pl.ds(b, 1), :] - (first - reach)
        inside = jnp.logical_and(slot >= 0, slot < span)
        target = jnp.where(inside, flds[pl.ds(b, 1), :] * span + slot, -1)
        present = seen[b] > 0

        @pl.when(jnp.logical_not(present))
        def _():
            mine[rows_of, :] = jnp.zeros((members, LANES), jnp.float32)
            other[rows_of, :] = jnp.zeros((members, LANES), jnp.float32)

        @pl.when(present)
        def _():
            wanted = jnp.broadcast_to(target, (members, LANES))
            index = jnp.broadcast_to(rws[pl.ds(b, 1), :], (members, LANES))
            for out, level in ((mine, core), (other, 1 - core)):
                total = jnp.zeros((members, LANES), jnp.float32)
                for f in range(fields):
                    for k in range(span):
                        slab = ahead[(f * levels + level) * span + k]
                        picked = jnp.take_along_axis(slab, index, axis=1)
                        total = jnp.where(wanted == f * span + k, picked, total)
                out[rows_of, :] = total

        return carry

    lax.fori_loop(0, batches, pick, 0)


def halves(x):
    high = x.astype(jnp.bfloat16)
    low = (x - high.astype(jnp.float32)).astype(jnp.bfloat16)
    return high, low


def analysis_kernel(count, place, table, info, *refs):
    arrived, rest = refs[:count], refs[count:]
    grid, from_left, from_right, out = rest[:4]
    local, remote, edges, spread_rows, spread_cols, vertical, position, sems = rest[4:]
    all_levels, length, _ = remote.shape
    slabs, members, rows = grid.shape
    fields, levels, columns = out.shape[1], out.shape[2], out.shape[3]
    groups = fields * levels
    batches = info.shape[0]
    total_cols = place[1].astype(jnp.float32)
    classes = table.shape[0]
    first = place[0].astype(jnp.float32)
    incoming = []
    level = 0
    for ref in arrived:
        for at in range(0, ref.shape[0], length):
            incoming.append((ref.at[at : at + length], remote.at[level]))
            level += 1
    incoming += [(grid, local), (from_left, edges.at[0]), (from_right, edges.at[1])]
    incoming = [
        pltpu.make_async_copy(ref, target, sems.at[slabs + n])
        for n, (ref, target) in enumerate(incoming)
    ]
    for copy in incoming:
        copy.start()
    for copy in incoming:
        copy.wait()
    for g in range(groups):
        for k in range(2):
            west, east = g * columns + k, g * columns + columns - 2 + k
            local[west] = local[west] + edges[0, g * 2 + k]
            local[east] = local[east] + edges[1, g * 2 + k]
    inverse = 1.0 / total_cols

    def widen(x):
        high, low = halves(x)
        return jnp.concatenate([high, high, low], axis=0)

    def spread_out(turn, weighted):
        change = jnp.dot(
            spread_rows[turn],
            jnp.concatenate(halves(weighted), axis=0),
            preferred_element_type=jnp.float32,
        )
        return change[:members] + change[members:]

    def covariance(turn, x):
        return jnp.dot(spread_cols[turn], widen(x), preferred_element_type=jnp.float32)

    def update(turn, x, weight):
        return x + spread_out(turn, covariance(turn, x) * weight)

    def rows_of(c):
        return pl.ds(pl.multiple_of(c * members, 8), members)

    def taper_to(turn, c):
        there = info[c]
        d_col = (there[0:1] - position[turn, 0]) * inverse
        d_row = (there[1:2] - position[turn, 1]) * (1.0 / RADY)
        radial = jnp.maximum(1.0 - d_col * d_col - d_row * d_row, 0.0)
        return radial * radial

    def analyse(turn, c, total):
        facts = info[c]
        priors = total * (1.0 / all_levels)
        average = jnp.sum(priors, axis=0, keepdims=True) * (1.0 / members)
        spread = priors - average
        variance = jnp.sum(spread * spread, axis=0, keepdims=True) / (members - 1) + EPSILON
        error = facts[4:5]
        ratio = 1.0 / (variance + error)
        shrink = variance * ratio
        factor = jnp.sqrt(error * ratio)
        increments = shrink * (facts[3:4] - average) + (factor - 1.0) * spread
        regress = spread / ((members - 1) * variance)
        high, low = halves(increments)
        spread_rows[turn, :members, :LANES] = high
        spread_rows[turn, :members, LANES:] = high
        spread_rows[turn, members:, :LANES] = low
        spread_rows[turn, members:, LANES:] = jnp.zeros_like(low)
        high = regress.astype(jnp.bfloat16).astype(jnp.float32)
        low = regress - high
        stacked = jnp.concatenate(
            [high, low, high, jnp.zeros((256 - 3 * members, LANES), jnp.float32)], axis=0
        )
        spread_cols[turn] = jnp.transpose(stacked)[:, : 3 * members].astype(jnp.bfloat16)

        def column_of(k):
            return jnp.transpose(jnp.broadcast_to(facts[k : k + 1], (LANES, LANES)))

        position[turn, 0] = column_of(0)
        position[turn, 1] = column_of(1)
        obs_class = column_of(2)
        for level in range(all_levels + levels):
            if level < all_levels:
                row = remote[level, batches * members : batches * members + 8, :]
                weights = [
                    jnp.broadcast_to(row[0:1, k : k + 1], (LANES, LANES)) for k in range(classes)
                ]
            else:
                weights = [table[k, level - all_levels] for k in range(classes)]
            chosen = jnp.zeros((LANES, LANES), jnp.float32) + weights[classes - 1]
            for k in range(classes - 1):
                chosen = jnp.where(obs_class == float(k), weights[k], chosen)
            vertical[turn, level] = chosen

    def batch(b, carry):
        turn = b % 2
        soon = jnp.minimum(b + 1, batches - 1)
        xs = [remote[g, rows_of(soon), :] for g in range(all_levels)]
        linked = covariance(turn, jnp.concatenate(xs, axis=1))
        weighted = linked[:, :LANES] * vertical[turn, 0]
        total = xs[0]
        for g in range(1, all_levels):
            weighted = weighted + linked[:, g * LANES : (g + 1) * LANES] * vertical[turn, g]
            total = total + xs[g]
        total = total + spread_out(turn, weighted * taper_to(turn, soon))

        lane = lax.broadcasted_iota(jnp.int32, (1, LANES), 1).astype(jnp.float32)
        d_row = (lane - position[turn, 1]) * (1.0 / RADY)
        across = 1.0 - d_row * d_row
        along = (first - position[turn, 0]) * inverse
        ats, ws = [], []
        for k in range(columns):
            d_col = along + k * inverse
            radial = jnp.maximum(across - d_col * d_col, 0.0)
            taper = radial * radial
            for level in range(levels):
                weight = taper * vertical[turn, all_levels + level]
                for f in range(fields):
                    ats.append((f * levels + level) * columns + k)
                    ws.append(weight)
        x = jnp.concatenate([local[at] for at in ats], axis=1)
        x = update(turn, x, jnp.concatenate(ws, axis=1))
        for i, at in enumerate(ats):
            local[at] = x[:, i * LANES : (i + 1) * LANES]
        analyse(1 - turn, soon, total)

        def later_many(c0, many):
            xs, ws, keep = [], [], []
            for k in range(many):
                theirs = rows_of(c0 + k)
                taper = taper_to(turn, c0 + k)
                for g in range(all_levels):
                    xs.append(remote[g, theirs, :])
                    ws.append(taper * vertical[turn, g])
                    keep.append((g, theirs))
            x = update(turn, jnp.concatenate(xs, axis=1), jnp.concatenate(ws, axis=1))
            for n, (g, theirs) in enumerate(keep):
                remote[g, theirs, :] = x[:, n * LANES : (n + 1) * LANES]

        count = jnp.maximum(batches - 2 - b, 0)

        for size in (1, 2):

            @pl.when((count // size) % 2 == 1)
            def _():
                later_many(b + 2 + (count % size), size)

        start = b + 2 + count % 4

        def four(i, carry):
            later_many(start + 4 * i, 4)
            return carry

        lax.fori_loop(0, count // 4, four, 0)
        return carry

    total = remote[0, 0:members, :]
    for level in range(1, all_levels):
        total = total + remote[level, 0:members, :]
    analyse(0, 0, total)
    lax.fori_loop(0, batches, batch, 0)
    outgoing = []
    for f in range(fields):
        for level in range(levels):
            for k in range(columns):
                at = (f * levels + level) * columns + k
                outgoing.append(
                    pltpu.make_async_copy(
                        local.at[at], out.at[:, f, level, k, :], sems.at[at]
                    )
                )
    for copy in outgoing:
        copy.start()
    for copy in outgoing:
        copy.wait()


def forecast(place, table, state, east, north, cols, rws, flds, length):
    members, fields, levels, columns, rows = state.shape
    groups = fields * levels
    smem = pl.BlockSpec(memory_space=pltpu.SMEM)
    vmem = pl.BlockSpec(memory_space=pltpu.VMEM)
    anywhere = pl.BlockSpec(memory_space=pl.ANY)
    picks = jax.ShapeDtypeStruct((length, LANES), jnp.float32)
    edge = jax.ShapeDtypeStruct((groups * 2, members, rows), jnp.float32)
    return pl.pallas_call(
        forecast_kernel,
        out_shape=(
            jax.ShapeDtypeStruct((groups * columns, members, rows), jnp.float32),
            edge,
            edge,
            picks,
            picks,
        ),
        in_specs=[smem, smem, anywhere] + [vmem] * 5,
        out_specs=(vmem,) * 5,
        scratch_shapes=[
            pltpu.VMEM((groups * columns, members, rows), jnp.float32),
            pltpu.VMEM((groups * (columns + 4), members, rows), jnp.float32),
            pltpu.SMEM((cols.shape[0],), jnp.int32),
            pltpu.SemaphoreType.DMA((groups * columns,)),
        ],
        compiler_params=pltpu.CompilerParams(vmem_limit_bytes=40 * 2**20),
    )(place, table, state, east, north, cols, rws, flds)


def assimilate(place, table, info, arrived, grid, from_left, from_right, shape, length):
    members, fields, levels, columns, rows = shape
    smem = pl.BlockSpec(memory_space=pltpu.SMEM)
    vmem = pl.BlockSpec(memory_space=pltpu.VMEM)
    anywhere = pl.BlockSpec(memory_space=pl.ANY)
    all_levels = sum(part.shape[0] for part in arrived) // length
    return pl.pallas_call(
        functools.partial(analysis_kernel, len(arrived)),
        out_shape=jax.ShapeDtypeStruct(shape, jnp.float32),
        in_specs=[smem, smem, vmem] + [anywhere] * (len(arrived) + 3),
        out_specs=anywhere,
        scratch_shapes=[
            pltpu.VMEM(grid.shape, jnp.float32),
            pltpu.VMEM((all_levels, length, LANES), jnp.float32),
            pltpu.VMEM((2,) + from_left.shape, jnp.float32),
            pltpu.VMEM((2, 2 * members, 2 * LANES), jnp.bfloat16),
            pltpu.VMEM((2, LANES, 3 * members), jnp.bfloat16),
            pltpu.VMEM((2, all_levels + levels, LANES, LANES), jnp.float32),
            pltpu.VMEM((2, 2, LANES, LANES), jnp.float32),
            pltpu.SemaphoreType.DMA((grid.shape[0] + all_levels + 3,)),
        ],
        compiler_params=pltpu.CompilerParams(vmem_limit_bytes=60 * 2**20),
    )(place, table, info, *arrived, grid, from_left, from_right)


def shards(
    state,
    eastward_current,
    northward_current,
    obs_col,
    obs_row,
    obs_field,
    obs_class,
    obs_value,
    obs_error,
    vertical_table,
):
    members, fields, levels, columns, rows = state.shape
    batches, obs = obs_col.shape
    homes = lax.axis_size("z") * lax.axis_size("y")
    tiles = homes * lax.axis_size("core")
    tile = lax.axis_index(TILES)
    core = lax.axis_index("core")
    first = tile * columns
    chunk = -(-(batches * members + 8) // (8 * homes)) * 8
    length = chunk * homes

    origin = (tile // 2 == 0).astype(jnp.int32)
    place = jnp.stack([first, core, origin, jnp.int32(tiles * columns)]).astype(jnp.int32)
    grid, to_left, to_right, mine, other = forecast(
        place, vertical_table, state, eastward_current, northward_current, obs_col, obs_row,
        obs_field, length,
    )

    swap = [(0, 1), (1, 0)]
    mine = mine + lax.ppermute(other, "core", swap)
    mine = lax.all_to_all(mine.reshape(homes, chunk, LANES), ("z", "y"), 0, 0, tiled=True)
    mine = jnp.sum(mine, axis=0)
    mine = lax.all_to_all(
        jnp.broadcast_to(mine[None], (homes, chunk, LANES)), ("z", "y"), 0, 0, tiled=True
    )
    mine = mine.reshape(length, LANES)

    ring = lax.axis_size("x")
    right = [(i, (i + 1) % ring) for i in range(ring)]
    left = [(j, i) for i, j in right]
    up = [(i, i + 1) for i in range(tiles - 1)]
    down = [(j, i) for i, j in up]
    mine, to_left, to_right = lax.optimization_barrier((mine, to_left, to_right))
    before = lax.ppermute(mine, "x", right)
    after = lax.ppermute(mine, "x", left)
    from_left = lax.ppermute(to_right, TILES, up)
    from_right = lax.ppermute(to_left, TILES, down)
    before, after, from_left, from_right = lax.optimization_barrier(
        (before, after, from_left, from_right)
    )
    across_a = lax.ppermute(after[: length // 2], "x", left)
    across_b = lax.ppermute(before[length // 2 :], "x", right)
    near = jnp.concatenate([mine, before, after], axis=0)
    across = jnp.concatenate([across_a, across_b], axis=0)
    arrived = [near, across]
    arrived += [lax.ppermute(part, "core", swap) for part in (near, across)]

    as_float = [v.astype(jnp.float32) for v in (obs_col, obs_row, obs_class)]
    blank = jnp.zeros_like(obs_value)
    info = jnp.stack([*as_float, obs_value, obs_error, blank, blank, blank], axis=1)
    where = jnp.stack([first, jnp.int32(tiles * columns)]).astype(jnp.int32)
    return assimilate(
        where, vertical_table, info, arrived, grid, from_left, from_right, state.shape, length
    )


def solution(mesh):
    fine = Mesh(mesh.devices.reshape(8, 8, 2, 4), ("z", "y", "core", "x"))
    state = P(None, None, "x", TILES, None)
    placed = (
        state,
        P("x", None),
        P("x", None),
        P(),
        P(),
        P(),
        P(),
        P(),
        P(),
        P(None, "x"),
    )
    return jax.shard_map(shards, mesh=fine, in_specs=placed, out_specs=state, check_vma=False)
```

```python
import functools

import jax
import jax.numpy as jnp
from jax import lax
from jax.experimental import pallas as pl
from jax.experimental.pallas import tpu as pltpu
from jax.sharding import Mesh, PartitionSpec as P

RADY = 40
KAPPA_COEF = 0.2
EPSILON = 1e-05
LANES = 128
TILES = ("z", "y", "core")


def forecast_kernel(
    place, table, state, east, north, cols, rws, flds, grid, to_left, to_right, mine, other,
    plain, ahead, seen, sems
):
    members, fields, levels, columns, rows = state.shape
    reach = 2
    batches = cols.shape[0]
    span = columns + 2 * reach
    groups = fields * levels
    first, core, origin, total_cols = place[0], place[1], place[2], place[3]
    copies = []
    for g in range(groups):
        for k in range(columns):
            slot = g * columns + k
            copies.append(
                pltpu.make_async_copy(
                    state.at[:, g // levels, g % levels, k, :], plain.at[slot], sems.at[slot]
                )
            )
    for copy in copies:
        copy.start()
    slot = cols[...] - (first - reach)
    near = jnp.where(jnp.logical_and(slot >= 0, slot < span), 1.0, 0.0)
    near = jnp.max(near, axis=1, keepdims=True)
    for b in range(batches):
        seen[b] = near[b, 0].astype(jnp.int32)
    lane = lax.broadcasted_iota(jnp.int32, (1, rows), 1)
    for g in range(groups):
        for k in range(columns):
            copies[g * columns + k].wait()
        l = g % levels
        zonal = 0.5 * east[l : l + 1, :]
        meridional = 0.5 * north[l : l + 1, :]
        to_east = KAPPA_COEF - zonal
        to_west = KAPPA_COEF + zonal
        to_north = jnp.where(lane == rows - 1, 0.0, KAPPA_COEF - meridional)
        to_south = jnp.where(lane == 0, 0.0, KAPPA_COEF + meridional)

        def step(west, here, east_):
            total = None
            if here is not None:
                total = (
                    (1.0 - 4.0 * KAPPA_COEF) * here
                    + to_north * pltpu.roll(here, rows - 1, 1)
                    + to_south * pltpu.roll(here, 1, 1)
                )
            if east_ is not None:
                total = to_east * east_ if total is None else total + to_east * east_
            if west is not None:
                total = to_west * west if total is None else total + to_west * west
            return total

        none = [None] * reach
        start = none + [plain[g * columns + k] for k in range(columns)] + none
        once = [None] * span
        for k in range(1, span - 1):
            value = step(start[k - 1], start[k], start[k + 1])
            if k < reach or k >= reach + columns:
                col = first + (k - reach)
                inside = jnp.logical_and(col >= 0, col < total_cols)
                value = jnp.where(inside, value, 0.0)
            once[k] = value
        for k in range(span):
            west = once[k - 1] if k > 0 else None
            east_ = once[k + 1] if k < span - 1 else None
            value = step(west, once[k], east_)
            ahead[g * span + k] = value
            if k < reach:
                to_left[g * reach + k] = value
            elif k < reach + columns:
                grid[g * columns + k - reach] = value
            else:
                to_right[g * reach + k - reach - columns] = value
    for out in (mine, other):
        out[batches * members :, :] = jnp.zeros(
            (out.shape[0] - batches * members, LANES), jnp.float32
        )
    vt = jnp.zeros((8, LANES), jnp.float32)
    spot = lax.broadcasted_iota(jnp.int32, (8, LANES), 1)
    for k in range(table.shape[0]):
        own_weight = jnp.where(core == 0, table[k, 0], table[k, 1])
        vt = jnp.where(spot == k, own_weight, vt)
    mine[batches * members : batches * members + 8, :] = jnp.where(origin == 1, vt, 0.0)

    def pick(b, carry):
        rows_of = pl.ds(pl.multiple_of(b * members, 8), members)
        slot = cols[pl.ds(b, 1), :] - (first - reach)
        inside = jnp.logical_and(slot >= 0, slot < span)
        target = jnp.where(inside, flds[pl.ds(b, 1), :] * span + slot, -1)
        present = seen[b] > 0

        @pl.when(jnp.logical_not(present))
        def _():
            mine[rows_of, :] = jnp.zeros((members, LANES), jnp.float32)
            other[rows_of, :] = jnp.zeros((members, LANES), jnp.float32)

        @pl.when(present)
        def _():
            wanted = jnp.broadcast_to(target, (members, LANES))
            index = jnp.broadcast_to(rws[pl.ds(b, 1), :], (members, LANES))
            for out, level in ((mine, core), (other, 1 - core)):
                total = jnp.zeros((members, LANES), jnp.float32)
                for f in range(fields):
                    for k in range(span):
                        slab = ahead[(f * levels + level) * span + k]
                        picked = jnp.take_along_axis(slab, index, axis=1)
                        total = jnp.where(wanted == f * span + k, picked, total)
                out[rows_of, :] = total

        return carry

    lax.fori_loop(0, batches, pick, 0)


def halves(x):
    high = x.astype(jnp.bfloat16)
    low = (x - high.astype(jnp.float32)).astype(jnp.bfloat16)
    return high, low


def analysis_kernel(count, place, table, info, *refs):
    arrived, rest = refs[:count], refs[count:]
    grid, from_left, from_right, out = rest[:4]
    local, remote, edges, spread_rows, spread_cols, vertical, position, sems = rest[4:]
    all_levels, length, _ = remote.shape
    slabs, members, rows = grid.shape
    fields, levels, columns = out.shape[1], out.shape[2], out.shape[3]
    groups = fields * levels
    batches = info.shape[0]
    total_cols = place[1].astype(jnp.float32)
    classes = table.shape[0]
    first = place[0].astype(jnp.float32)
    incoming = []
    around = place[2]
    ring = all_levels // 2
    for n, ref in enumerate(arrived):
        for part in range(ring):
            level = part
            if n < 2:
                level = lax.rem(around + (0, ring - 1, 1, 2)[part], ring)
            rows_in = slice(0, ref.shape[1]) if n >= 2 else slice(length - ref.shape[1], length)
            incoming.append((ref.at[part], remote.at[(n % 2) * ring + level, rows_in]))
    incoming += [(grid, local), (from_left, edges.at[0]), (from_right, edges.at[1])]
    incoming = [
        pltpu.make_async_copy(ref, target, sems.at[slabs + n])
        for n, (ref, target) in enumerate(incoming)
    ]
    for copy in incoming:
        copy.start()
    for copy in incoming:
        copy.wait()
    for g in range(groups):
        for k in range(2):
            west, east = g * columns + k, g * columns + columns - 2 + k
            local[west] = local[west] + edges[0, g * 2 + k]
            local[east] = local[east] + edges[1, g * 2 + k]
    inverse = 1.0 / total_cols

    def widen(x):
        high, low = halves(x)
        return jnp.concatenate([high, high, low], axis=0)

    def spread_out(turn, weighted):
        change = jnp.dot(
            spread_rows[turn],
            jnp.concatenate(halves(weighted), axis=0),
            preferred_element_type=jnp.float32,
        )
        return change[:members] + change[members:]

    def covariance(turn, x):
        return jnp.dot(spread_cols[turn], widen(x), preferred_element_type=jnp.float32)

    def update(turn, x, weight):
        return x + spread_out(turn, covariance(turn, x) * weight)

    def rows_of(c):
        return pl.ds(pl.multiple_of(c * members, 8), members)

    def taper_to(turn, c):
        there = info[c]
        d_col = (there[0:1] - position[turn, 0]) * inverse
        d_row = (there[1:2] - position[turn, 1]) * (1.0 / RADY)
        radial = jnp.maximum(1.0 - d_col * d_col - d_row * d_row, 0.0)
        return radial * radial

    def analyse(turn, c, total):
        facts = info[c]
        priors = total * (1.0 / all_levels)
        average = jnp.sum(priors, axis=0, keepdims=True) * (1.0 / members)
        spread = priors - average
        variance = jnp.sum(spread * spread, axis=0, keepdims=True) / (members - 1) + EPSILON
        error = facts[4:5]
        ratio = 1.0 / (variance + error)
        shrink = variance * ratio
        factor = jnp.sqrt(error * ratio)
        increments = shrink * (facts[3:4] - average) + (factor - 1.0) * spread
        regress = spread / ((members - 1) * variance)
        high, low = halves(increments)
        spread_rows[turn, :members, :LANES] = high
        spread_rows[turn, :members, LANES:] = high
        spread_rows[turn, members:, :LANES] = low
        spread_rows[turn, members:, LANES:] = jnp.zeros_like(low)
        high = regress.astype(jnp.bfloat16).astype(jnp.float32)
        low = regress - high
        stacked = jnp.concatenate(
            [high, low, high, jnp.zeros((256 - 3 * members, LANES), jnp.float32)], axis=0
        )
        spread_cols[turn] = jnp.transpose(stacked)[:, : 3 * members].astype(jnp.bfloat16)

        def column_of(k):
            return jnp.transpose(jnp.broadcast_to(facts[k : k + 1], (LANES, LANES)))

        position[turn, 0] = column_of(0)
        position[turn, 1] = column_of(1)
        obs_class = column_of(2)
        for level in range(all_levels + levels):
            if level < all_levels:
                row = remote[level, batches * members : batches * members + 8, :]
                weights = [
                    jnp.broadcast_to(row[0:1, k : k + 1], (LANES, LANES)) for k in range(classes)
                ]
            else:
                weights = [table[k, level - all_levels] for k in range(classes)]
            chosen = jnp.zeros((LANES, LANES), jnp.float32) + weights[classes - 1]
            for k in range(classes - 1):
                chosen = jnp.where(obs_class == float(k), weights[k], chosen)
            vertical[turn, level] = chosen

    def batch(b, carry):
        turn = b % 2
        soon = jnp.minimum(b + 1, batches - 1)
        xs = [remote[g, rows_of(soon), :] for g in range(all_levels)]
        linked = covariance(turn, jnp.concatenate(xs, axis=1))
        weighted = linked[:, :LANES] * vertical[turn, 0]
        total = xs[0]
        for g in range(1, all_levels):
            weighted = weighted + linked[:, g * LANES : (g + 1) * LANES] * vertical[turn, g]
            total = total + xs[g]
        total = total + spread_out(turn, weighted * taper_to(turn, soon))

        lane = lax.broadcasted_iota(jnp.int32, (1, LANES), 1).astype(jnp.float32)
        d_row = (lane - position[turn, 1]) * (1.0 / RADY)
        across = 1.0 - d_row * d_row
        along = (first - position[turn, 0]) * inverse
        ats, ws = [], []
        for k in range(columns):
            d_col = along + k * inverse
            radial = jnp.maximum(across - d_col * d_col, 0.0)
            taper = radial * radial
            for level in range(levels):
                weight = taper * vertical[turn, all_levels + level]
                for f in range(fields):
                    ats.append((f * levels + level) * columns + k)
                    ws.append(weight)
        x = jnp.concatenate([local[at] for at in ats], axis=1)
        x = update(turn, x, jnp.concatenate(ws, axis=1))
        for i, at in enumerate(ats):
            local[at] = x[:, i * LANES : (i + 1) * LANES]
        analyse(1 - turn, soon, total)

        def later_many(c0, many):
            xs, ws, keep = [], [], []
            for k in range(many):
                theirs = rows_of(c0 + k)
                taper = taper_to(turn, c0 + k)
                for g in range(all_levels):
                    xs.append(remote[g, theirs, :])
                    ws.append(taper * vertical[turn, g])
                    keep.append((g, theirs))
            x = update(turn, jnp.concatenate(xs, axis=1), jnp.concatenate(ws, axis=1))
            for n, (g, theirs) in enumerate(keep):
                remote[g, theirs, :] = x[:, n * LANES : (n + 1) * LANES]

        count = jnp.maximum(batches - 2 - b, 0)

        for size in (1, 2):

            @pl.when((count // size) % 2 == 1)
            def _():
                later_many(b + 2 + (count % size), size)

        start = b + 2 + count % 4

        def four(i, carry):
            later_many(start + 4 * i, 4)
            return carry

        lax.fori_loop(0, count // 4, four, 0)
        return carry

    total = remote[0, 0:members, :]
    for level in range(1, all_levels):
        total = total + remote[level, 0:members, :]
    analyse(0, 0, total)
    lax.fori_loop(0, batches, batch, 0)
    outgoing = []
    for f in range(fields):
        for level in range(levels):
            for k in range(columns):
                at = (f * levels + level) * columns + k
                outgoing.append(
                    pltpu.make_async_copy(
                        local.at[at], out.at[:, f, level, k, :], sems.at[at]
                    )
                )
    for copy in outgoing:
        copy.start()
    for copy in outgoing:
        copy.wait()


def forecast(place, table, state, east, north, cols, rws, flds, length):
    members, fields, levels, columns, rows = state.shape
    groups = fields * levels
    smem = pl.BlockSpec(memory_space=pltpu.SMEM)
    vmem = pl.BlockSpec(memory_space=pltpu.VMEM)
    anywhere = pl.BlockSpec(memory_space=pl.ANY)
    picks = jax.ShapeDtypeStruct((length, LANES), jnp.float32)
    edge = jax.ShapeDtypeStruct((groups * 2, members, rows), jnp.float32)
    return pl.pallas_call(
        forecast_kernel,
        out_shape=(
            jax.ShapeDtypeStruct((groups * columns, members, rows), jnp.float32),
            edge,
            edge,
            picks,
            picks,
        ),
        in_specs=[smem, smem, anywhere] + [vmem] * 5,
        out_specs=(vmem,) * 5,
        scratch_shapes=[
            pltpu.VMEM((groups * columns, members, rows), jnp.float32),
            pltpu.VMEM((groups * (columns + 4), members, rows), jnp.float32),
            pltpu.SMEM((cols.shape[0],), jnp.int32),
            pltpu.SemaphoreType.DMA((groups * columns,)),
        ],
        compiler_params=pltpu.CompilerParams(vmem_limit_bytes=40 * 2**20),
    )(place, table, state, east, north, cols, rws, flds)


def assimilate(place, table, info, arrived, grid, from_left, from_right, shape, length):
    members, fields, levels, columns, rows = shape
    smem = pl.BlockSpec(memory_space=pltpu.SMEM)
    vmem = pl.BlockSpec(memory_space=pltpu.VMEM)
    anywhere = pl.BlockSpec(memory_space=pl.ANY)
    all_levels = 2 * arrived[0].shape[0]
    return pl.pallas_call(
        functools.partial(analysis_kernel, len(arrived)),
        out_shape=jax.ShapeDtypeStruct(shape, jnp.float32),
        in_specs=[smem, smem, vmem] + [anywhere] * (len(arrived) + 3),
        out_specs=anywhere,
        scratch_shapes=[
            pltpu.VMEM(grid.shape, jnp.float32),
            pltpu.VMEM((all_levels, length, LANES), jnp.float32),
            pltpu.VMEM((2,) + from_left.shape, jnp.float32),
            pltpu.VMEM((2, 2 * members, 2 * LANES), jnp.bfloat16),
            pltpu.VMEM((2, LANES, 3 * members), jnp.bfloat16),
            pltpu.VMEM((2, all_levels + levels, LANES, LANES), jnp.float32),
            pltpu.VMEM((2, 2, LANES, LANES), jnp.float32),
            pltpu.SemaphoreType.DMA((grid.shape[0] + 2 * all_levels + 3,)),
        ],
        compiler_params=pltpu.CompilerParams(vmem_limit_bytes=28 * 2**20),
    )(place, table, info, *arrived, grid, from_left, from_right)


def shards(
    state,
    eastward_current,
    northward_current,
    obs_col,
    obs_row,
    obs_field,
    obs_class,
    obs_value,
    obs_error,
    vertical_table,
):
    members, fields, levels, columns, rows = state.shape
    batches, obs = obs_col.shape
    homes = lax.axis_size("z") * lax.axis_size("y")
    tiles = homes * lax.axis_size("core")
    tile = lax.axis_index(TILES)
    core = lax.axis_index("core")
    first = tile * columns
    chunk = -(-(batches * members + 8) // (8 * homes)) * 8
    length = chunk * homes

    origin = (tile // 2 == 0).astype(jnp.int32)
    place = jnp.stack([first, core, origin, jnp.int32(tiles * columns)]).astype(jnp.int32)
    grid, to_left, to_right, mine, other = forecast(
        place, vertical_table, state, eastward_current, northward_current, obs_col, obs_row,
        obs_field, length,
    )

    swap = [(0, 1), (1, 0)]
    mine = mine + lax.ppermute(other, "core", swap)
    mine = lax.all_to_all(mine.reshape(homes, chunk, LANES), ("z", "y"), 0, 0, tiled=True)
    mine = jnp.sum(mine, axis=0)
    mine = lax.all_to_all(
        jnp.broadcast_to(mine[None], (homes, chunk, LANES)), ("z", "y"), 0, 0, tiled=True
    )
    mine = mine.reshape(length, LANES)

    ring = lax.axis_size("x")
    right = [(i, (i + 1) % ring) for i in range(ring)]
    left = [(j, i) for i, j in right]
    up = [(i, i + 1) for i in range(tiles - 1)]
    down = [(j, i) for i, j in up]
    cut = 640
    used = batches * members + 8
    middle = (used - cut) // 16 * 8
    mine, to_left, to_right = lax.optimization_barrier((mine, to_left, to_right))
    first_rows = lax.all_gather(mine[:cut], "x")
    last_rows = mine[cut:used]
    before = lax.ppermute(last_rows, "x", right)
    after = lax.ppermute(last_rows, "x", left)
    from_left = lax.ppermute(to_right, TILES, up)
    from_right = lax.ppermute(to_left, TILES, down)
    across_a = lax.ppermute(after[:middle], "x", left)
    across_b = lax.ppermute(before[middle:], "x", right)
    last_rows = jnp.concatenate([last_rows, before, after, across_a, across_b], axis=0)
    last_rows = last_rows.reshape(ring, used - cut, LANES)
    last_swapped = lax.ppermute(last_rows, "core", swap)
    first_rows, last_rows, from_left, from_right = lax.optimization_barrier(
        (first_rows, last_rows, from_left, from_right)
    )
    arrived = [last_rows, last_swapped]
    arrived += [first_rows, lax.ppermute(first_rows, "core", swap)]

    as_float = [v.astype(jnp.float32) for v in (obs_col, obs_row, obs_class)]
    blank = jnp.zeros_like(obs_value)
    info = jnp.stack([*as_float, obs_value, obs_error, blank, blank, blank], axis=1)
    where = jnp.stack([first, jnp.int32(tiles * columns), lax.axis_index("x")]).astype(jnp.int32)
    return assimilate(
        where, vertical_table, info, arrived, grid, from_left, from_right, state.shape, used
    )


def solution(mesh):
    fine = Mesh(mesh.devices.reshape(8, 8, 2, 4), ("z", "y", "core", "x"))
    state = P(None, None, "x", TILES, None)
    placed = (
        state,
        P("x", None),
        P("x", None),
        P(),
        P(),
        P(),
        P(),
        P(),
        P(),
        P(None, "x"),
    )
    return jax.shard_map(shards, mesh=fine, in_specs=placed, out_specs=state, check_vma=False)
```

```python
import functools

import jax
import jax.numpy as jnp
from jax import lax
from jax.experimental import pallas as pl
from jax.experimental.pallas import tpu as pltpu
from jax.sharding import Mesh, PartitionSpec as P

RADY = 40
KAPPA_COEF = 0.2
EPSILON = 1e-05
LANES = 128
TILES = ("z", "y", "core")


def forecast_kernel(
    place, table, state, east_in, north_in, cols_in, rws_in, flds_in,
    grid, to_left, to_right, mine, other,
    whole, east, north, cols, rws, flds, plain, ahead, seen, sems,
):
    members, fields, levels, columns, rows = state.shape
    reach = 2
    batches = cols.shape[0]
    span = columns + 2 * reach
    groups = fields * levels
    first, core, origin, total_cols = place[0], place[1], place[2], place[3]
    small = ((east_in, east), (north_in, north), (cols_in, cols), (rws_in, rws), (flds_in, flds))
    slots = groups * columns
    fetches = [
        pltpu.make_async_copy(source, target, sems.at[slots + n])
        for n, (source, target) in enumerate(((state, whole),) + small)
    ]
    for fetch in fetches:
        fetch.start()
    for fetch in fetches:
        fetch.wait()
    copies = []
    for g in range(groups):
        for k in range(columns):
            slot = g * columns + k
            copies.append(
                pltpu.make_async_copy(
                    whole.at[:, g // levels, g % levels, k, :], plain.at[slot], sems.at[slot]
                )
            )
    for copy in copies:
        copy.start()
    slot = cols[...] - (first - reach)
    near = jnp.where(jnp.logical_and(slot >= 0, slot < span), 1.0, 0.0)
    near = jnp.max(near, axis=1, keepdims=True)
    for b in range(batches):
        seen[b] = near[b, 0].astype(jnp.int32)
    lane = lax.broadcasted_iota(jnp.int32, (1, rows), 1)
    for g in range(groups):
        for k in range(columns):
            copies[g * columns + k].wait()
        l = g % levels
        zonal = 0.5 * east[l : l + 1, :]
        meridional = 0.5 * north[l : l + 1, :]
        to_east = KAPPA_COEF - zonal
        to_west = KAPPA_COEF + zonal
        to_north = jnp.where(lane == rows - 1, 0.0, KAPPA_COEF - meridional)
        to_south = jnp.where(lane == 0, 0.0, KAPPA_COEF + meridional)

        def step(west, here, east_):
            total = None
            if here is not None:
                total = (
                    (1.0 - 4.0 * KAPPA_COEF) * here
                    + to_north * pltpu.roll(here, rows - 1, 1)
                    + to_south * pltpu.roll(here, 1, 1)
                )
            if east_ is not None:
                total = to_east * east_ if total is None else total + to_east * east_
            if west is not None:
                total = to_west * west if total is None else total + to_west * west
            return total

        none = [None] * reach
        start = none + [plain[g * columns + k] for k in range(columns)] + none
        once = [None] * span
        for k in range(1, span - 1):
            value = step(start[k - 1], start[k], start[k + 1])
            if k < reach or k >= reach + columns:
                col = first + (k - reach)
                inside = jnp.logical_and(col >= 0, col < total_cols)
                value = jnp.where(inside, value, 0.0)
            once[k] = value
        for k in range(span):
            west = once[k - 1] if k > 0 else None
            east_ = once[k + 1] if k < span - 1 else None
            value = step(west, once[k], east_)
            ahead[g * span + k] = value
            if k < reach:
                to_left[g * reach + k] = value
            elif k < reach + columns:
                grid[g * columns + k - reach] = value
            else:
                to_right[g * reach + k - reach - columns] = value
    for out in (mine, other):
        out[batches * members :, :] = jnp.zeros(
            (out.shape[0] - batches * members, LANES), jnp.float32
        )
    vt = jnp.zeros((8, LANES), jnp.float32)
    spot = lax.broadcasted_iota(jnp.int32, (8, LANES), 1)
    for k in range(table.shape[1]):
        own_weight = jnp.where(core == 0, table[0, k], table[1, k])
        vt = jnp.where(spot == k, own_weight, vt)
    mine[batches * members : batches * members + 8, :] = jnp.where(origin == 1, vt, 0.0)

    def pick(b, carry):
        rows_of = pl.ds(pl.multiple_of(b * members, 8), members)
        slot = cols[pl.ds(b, 1), :] - (first - reach)
        inside = jnp.logical_and(slot >= 0, slot < span)
        target = jnp.where(inside, flds[pl.ds(b, 1), :] * span + slot, -1)
        present = seen[b] > 0

        @pl.when(jnp.logical_not(present))
        def _():
            mine[rows_of, :] = jnp.zeros((members, LANES), jnp.float32)
            other[rows_of, :] = jnp.zeros((members, LANES), jnp.float32)

        @pl.when(present)
        def _():
            wanted = jnp.broadcast_to(target, (members, LANES))
            index = jnp.broadcast_to(rws[pl.ds(b, 1), :], (members, LANES))
            for out, level in ((mine, core), (other, 1 - core)):
                total = jnp.zeros((members, LANES), jnp.float32)
                for f in range(fields):
                    for k in range(span):
                        slab = ahead[(f * levels + level) * span + k]
                        picked = jnp.take_along_axis(slab, index, axis=1)
                        total = jnp.where(wanted == f * span + k, picked, total)
                out[rows_of, :] = total

        return carry

    lax.fori_loop(0, batches, pick, 0)


def halves(x):
    high = x.astype(jnp.bfloat16)
    low = (x - high.astype(jnp.float32)).astype(jnp.bfloat16)
    return high, low


def analysis_kernel(count, place, table, *refs):
    info, refs = refs[:5], refs[5:]
    arrived, rest = refs[:count], refs[count:]
    grid, from_left, from_right, out = rest[:4]
    local, remote, edges, spread_rows, spread_cols, vertical, position, sems = rest[4:]
    all_levels, length, _ = remote.shape
    slabs, members, rows = grid.shape
    fields, levels, columns = out.shape[1], out.shape[2], out.shape[3]
    groups = fields * levels
    batches = info[0].shape[0]
    total_cols = place[1].astype(jnp.float32)
    classes = table.shape[1]
    first = place[0].astype(jnp.float32)
    incoming = []
    around = place[2]
    ring = all_levels // 2
    for n, ref in enumerate(arrived):
        for part in range(ring):
            level = part
            if n < 2:
                level = lax.rem(around + (0, ring - 1, 1, 2)[part], ring)
            rows_in = slice(0, ref.shape[1]) if n >= 2 else slice(length - ref.shape[1], length)
            incoming.append((ref.at[part], remote.at[(n % 2) * ring + level, rows_in]))
    incoming += [(grid, local), (from_left, edges.at[0]), (from_right, edges.at[1])]
    incoming = [
        pltpu.make_async_copy(ref, target, sems.at[slabs + n])
        for n, (ref, target) in enumerate(incoming)
    ]
    for copy in incoming:
        copy.start()
    for copy in incoming:
        copy.wait()
    for g in range(groups):
        for k in range(2):
            west, east = g * columns + k, g * columns + columns - 2 + k
            local[west] = local[west] + edges[0, g * 2 + k]
            local[east] = local[east] + edges[1, g * 2 + k]
    inverse = 1.0 / total_cols

    def widen(x):
        high, low = halves(x)
        return jnp.concatenate([high, high, low], axis=0)

    def spread_out(turn, weighted):
        change = jnp.dot(
            spread_rows[turn],
            jnp.concatenate(halves(weighted), axis=0),
            preferred_element_type=jnp.float32,
        )
        return change[:members] + change[members:]

    def covariance(turn, x):
        return jnp.dot(spread_cols[turn], widen(x), preferred_element_type=jnp.float32)

    def update(turn, x, weight):
        return x + spread_out(turn, covariance(turn, x) * weight)

    def rows_of(c):
        return pl.ds(pl.multiple_of(c * members, 8), members)

    def fact(k, c):
        return info[k][pl.ds(c, 1), :].astype(jnp.float32)

    def taper_to(turn, c):
        d_col = (fact(0, c) - position[turn, 0]) * inverse
        d_row = (fact(1, c) - position[turn, 1]) * (1.0 / RADY)
        radial = jnp.maximum(1.0 - d_col * d_col - d_row * d_row, 0.0)
        return radial * radial

    def analyse(turn, c, total):
        priors = total * (1.0 / all_levels)
        average = jnp.sum(priors, axis=0, keepdims=True) * (1.0 / members)
        spread = priors - average
        variance = jnp.sum(spread * spread, axis=0, keepdims=True) / (members - 1) + EPSILON
        error = fact(4, c)
        ratio = 1.0 / (variance + error)
        shrink = variance * ratio
        factor = jnp.sqrt(error * ratio)
        increments = shrink * (fact(3, c) - average) + (factor - 1.0) * spread
        regress = spread / ((members - 1) * variance)
        high, low = halves(increments)
        spread_rows[turn, :members, :LANES] = high
        spread_rows[turn, :members, LANES:] = high
        spread_rows[turn, members:, :LANES] = low
        spread_rows[turn, members:, LANES:] = jnp.zeros_like(low)
        high = regress.astype(jnp.bfloat16).astype(jnp.float32)
        low = regress - high
        stacked = jnp.concatenate(
            [high, low, high, jnp.zeros((256 - 3 * members, LANES), jnp.float32)], axis=0
        )
        spread_cols[turn] = jnp.transpose(stacked)[:, : 3 * members].astype(jnp.bfloat16)

        def column_of(k):
            return jnp.transpose(jnp.broadcast_to(fact(k, c), (LANES, LANES)))

        position[turn, 0] = column_of(0)
        position[turn, 1] = column_of(1)
        obs_class = column_of(2)
        for level in range(all_levels + levels):
            if level < all_levels:
                row = remote[level, batches * members : batches * members + 8, :]
                weights = [
                    jnp.broadcast_to(row[0:1, k : k + 1], (LANES, LANES)) for k in range(classes)
                ]
            else:
                weights = [table[level - all_levels, k] for k in range(classes)]
            chosen = jnp.zeros((LANES, LANES), jnp.float32) + weights[classes - 1]
            for k in range(classes - 1):
                chosen = jnp.where(obs_class == float(k), weights[k], chosen)
            vertical[turn, level] = chosen

    def batch(b, carry):
        turn = b % 2
        soon = jnp.minimum(b + 1, batches - 1)
        xs = [remote[g, rows_of(soon), :] for g in range(all_levels)]
        linked = covariance(turn, jnp.concatenate(xs, axis=1))
        weighted = linked[:, :LANES] * vertical[turn, 0]
        total = xs[0]
        for g in range(1, all_levels):
            weighted = weighted + linked[:, g * LANES : (g + 1) * LANES] * vertical[turn, g]
            total = total + xs[g]
        total = total + spread_out(turn, weighted * taper_to(turn, soon))

        lane = lax.broadcasted_iota(jnp.int32, (1, LANES), 1).astype(jnp.float32)
        d_row = (lane - position[turn, 1]) * (1.0 / RADY)
        across = 1.0 - d_row * d_row
        along = (first - position[turn, 0]) * inverse
        ats, ws = [], []
        for k in range(columns):
            d_col = along + k * inverse
            radial = jnp.maximum(across - d_col * d_col, 0.0)
            taper = radial * radial
            for level in range(levels):
                weight = taper * vertical[turn, all_levels + level]
                for f in range(fields):
                    ats.append((f * levels + level) * columns + k)
                    ws.append(weight)
        x = jnp.concatenate([local[at] for at in ats], axis=1)
        x = update(turn, x, jnp.concatenate(ws, axis=1))
        for i, at in enumerate(ats):
            local[at] = x[:, i * LANES : (i + 1) * LANES]
        analyse(1 - turn, soon, total)

        def later_many(c0, many):
            xs, ws, keep = [], [], []
            for k in range(many):
                theirs = rows_of(c0 + k)
                taper = taper_to(turn, c0 + k)
                for g in range(all_levels):
                    xs.append(remote[g, theirs, :])
                    ws.append(taper * vertical[turn, g])
                    keep.append((g, theirs))
            x = update(turn, jnp.concatenate(xs, axis=1), jnp.concatenate(ws, axis=1))
            for n, (g, theirs) in enumerate(keep):
                remote[g, theirs, :] = x[:, n * LANES : (n + 1) * LANES]

        count = jnp.maximum(batches - 2 - b, 0)

        for size in (1, 2):

            @pl.when((count // size) % 2 == 1)
            def _():
                later_many(b + 2 + (count % size), size)

        start = b + 2 + count % 4

        def four(i, carry):
            later_many(start + 4 * i, 4)
            return carry

        lax.fori_loop(0, count // 4, four, 0)
        return carry

    total = remote[0, 0:members, :]
    for level in range(1, all_levels):
        total = total + remote[level, 0:members, :]
    analyse(0, 0, total)
    lax.fori_loop(0, batches, batch, 0)
    outgoing = []
    for f in range(fields):
        for level in range(levels):
            for k in range(columns):
                at = (f * levels + level) * columns + k
                outgoing.append(
                    pltpu.make_async_copy(
                        local.at[at], out.at[:, f, level, k, :], sems.at[at]
                    )
                )
    for copy in outgoing:
        copy.start()
    for copy in outgoing:
        copy.wait()


def forecast(place, table, state, east, north, cols, rws, flds, length):
    members, fields, levels, columns, rows = state.shape
    groups = fields * levels
    smem = pl.BlockSpec(memory_space=pltpu.SMEM)
    vmem = pl.BlockSpec(memory_space=pltpu.VMEM)
    anywhere = pl.BlockSpec(memory_space=pl.ANY)
    picks = jax.ShapeDtypeStruct((length, LANES), jnp.float32)
    edge = jax.ShapeDtypeStruct((groups * 2, members, rows), jnp.float32)
    return pl.pallas_call(
        forecast_kernel,
        out_shape=(
            jax.ShapeDtypeStruct((groups * columns, members, rows), jnp.float32),
            edge,
            edge,
            picks,
            picks,
        ),
        in_specs=[smem, smem] + [anywhere] * 6,
        out_specs=(vmem,) * 5,
        scratch_shapes=[pltpu.VMEM(v.shape, v.dtype) for v in (state, east, north, cols, rws, flds)]
        + [
            pltpu.VMEM((groups * columns, members, rows), jnp.float32),
            pltpu.VMEM((groups * (columns + 4), members, rows), jnp.float32),
            pltpu.SMEM((cols.shape[0],), jnp.int32),
            pltpu.SemaphoreType.DMA((groups * columns + 6,)),
        ],
        compiler_params=pltpu.CompilerParams(vmem_limit_bytes=60 * 2**20),
    )(place, table, state, east, north, cols, rws, flds)


def assimilate(place, table, info, arrived, grid, from_left, from_right, shape, length):
    members, fields, levels, columns, rows = shape
    smem = pl.BlockSpec(memory_space=pltpu.SMEM)
    vmem = pl.BlockSpec(memory_space=pltpu.VMEM)
    anywhere = pl.BlockSpec(memory_space=pl.ANY)
    all_levels = 2 * arrived[0].shape[0]
    return pl.pallas_call(
        functools.partial(analysis_kernel, len(arrived)),
        out_shape=jax.ShapeDtypeStruct(shape, jnp.float32),
        in_specs=[smem, smem] + [vmem] * len(info) + [anywhere] * (len(arrived) + 3),
        out_specs=anywhere,
        scratch_shapes=[
            pltpu.VMEM(grid.shape, jnp.float32),
            pltpu.VMEM((all_levels, length, LANES), jnp.float32),
            pltpu.VMEM((2,) + from_left.shape, jnp.float32),
            pltpu.VMEM((2, 2 * members, 2 * LANES), jnp.bfloat16),
            pltpu.VMEM((2, LANES, 3 * members), jnp.bfloat16),
            pltpu.VMEM((2, all_levels + levels, LANES, LANES), jnp.float32),
            pltpu.VMEM((2, 2, LANES, LANES), jnp.float32),
            pltpu.SemaphoreType.DMA((grid.shape[0] + 2 * all_levels + 3,)),
        ],
        compiler_params=pltpu.CompilerParams(vmem_limit_bytes=60 * 2**20),
    )(place, table, *info, *arrived, grid, from_left, from_right)


def shards(
    state,
    eastward_current,
    northward_current,
    obs_col,
    obs_row,
    obs_field,
    obs_class,
    obs_value,
    obs_error,
    vertical_table,
):
    members, fields, levels, columns, rows = state.shape
    batches, obs = obs_col.shape
    homes = lax.axis_size("z") * lax.axis_size("y")
    tiles = homes * lax.axis_size("core")
    tile = lax.axis_index(TILES)
    core = lax.axis_index("core")
    first = tile * columns
    chunk = -(-(batches * members + 8) // (8 * homes)) * 8
    length = chunk * homes

    table = vertical_table.T
    origin = (tile // 2 == 0).astype(jnp.int32)
    place = jnp.stack([first, core, origin, jnp.int32(tiles * columns)]).astype(jnp.int32)
    grid, to_left, to_right, mine, other = forecast(
        place, table, state, eastward_current, northward_current, obs_col, obs_row,
        obs_field, length,
    )

    swap = [(0, 1), (1, 0)]
    mine = mine + lax.ppermute(other, "core", swap)
    mine = lax.all_to_all(mine.reshape(homes, chunk, LANES), ("z", "y"), 0, 0, tiled=True)
    mine = jnp.sum(mine, axis=0)
    mine = lax.all_to_all(
        jnp.broadcast_to(mine[None], (homes, chunk, LANES)), ("z", "y"), 0, 0, tiled=True
    )
    mine = mine.reshape(length, LANES)

    ring = lax.axis_size("x")
    right = [(i, (i + 1) % ring) for i in range(ring)]
    left = [(j, i) for i, j in right]
    up = [(i, i + 1) for i in range(tiles - 1)]
    down = [(j, i) for i, j in up]
    cut = 640
    used = batches * members + 8
    middle = (used - cut) // 16 * 8
    mine, to_left, to_right = lax.optimization_barrier((mine, to_left, to_right))
    first_rows = lax.all_gather(mine[:cut], "x")
    last_rows = mine[cut:used]
    before = lax.ppermute(last_rows, "x", right)
    after = lax.ppermute(last_rows, "x", left)
    from_left = lax.ppermute(to_right, TILES, up)
    from_right = lax.ppermute(to_left, TILES, down)
    across_a = lax.ppermute(after[:middle], "x", left)
    across_b = lax.ppermute(before[middle:], "x", right)
    last_rows = jnp.concatenate([last_rows, before, after, across_a, across_b], axis=0)
    last_rows = last_rows.reshape(ring, used - cut, LANES)
    last_swapped = lax.ppermute(last_rows, "core", swap)
    first_rows, last_rows, from_left, from_right = lax.optimization_barrier(
        (first_rows, last_rows, from_left, from_right)
    )
    arrived = [last_rows, last_swapped]
    arrived += [first_rows, lax.ppermute(first_rows, "core", swap)]

    facts = [obs_col, obs_row, obs_class, obs_value, obs_error]
    where = jnp.stack([first, jnp.int32(tiles * columns), lax.axis_index("x")]).astype(jnp.int32)
    return assimilate(
        where, table, facts, arrived, grid, from_left, from_right, state.shape, used
    )


def solution(mesh):
    fine = Mesh(mesh.devices.reshape(8, 8, 2, 4), ("z", "y", "core", "x"))
    state = P(None, None, "x", TILES, None)
    placed = (
        state,
        P("x", None),
        P("x", None),
        P(),
        P(),
        P(),
        P(),
        P(),
        P(),
        P(None, "x"),
    )
    return jax.shard_map(shards, mesh=fine, in_specs=placed, out_specs=state, check_vma=False)
```

```python
import functools

import jax
import jax.numpy as jnp
from jax import lax
from jax.experimental import pallas as pl
from jax.experimental.pallas import tpu as pltpu
from jax.sharding import Mesh, PartitionSpec as P

RADY = 40
KAPPA_COEF = 0.2
EPSILON = 1e-05
LANES = 128
TILES = ("z", "y", "core")


def forecast_kernel(
    place, table, state, east, north, cols, rws, flds, grid, to_left, to_right, mine, other,
    plain, ahead, seen, sems
):
    members, fields, levels, columns, rows = state.shape
    reach = 2
    batches = cols.shape[0]
    span = columns + 2 * reach
    groups = fields * levels
    first, core, origin, total_cols = place[0], place[1], place[2], place[3]
    copies = []
    for g in range(groups):
        for k in range(columns):
            slot = g * columns + k
            copies.append(
                pltpu.make_async_copy(
                    state.at[:, g // levels, g % levels, k, :], plain.at[slot], sems.at[slot]
                )
            )
    for copy in copies:
        copy.start()
    slot = cols[...] - (first - reach)
    near = jnp.where(jnp.logical_and(slot >= 0, slot < span), 1.0, 0.0)
    near = jnp.max(near, axis=1, keepdims=True)
    for b in range(batches):
        seen[b] = near[b, 0].astype(jnp.int32)
    lane = lax.broadcasted_iota(jnp.int32, (1, rows), 1)
    for g in range(groups):
        for k in range(columns):
            copies[g * columns + k].wait()
        l = g % levels
        zonal = 0.5 * east[l : l + 1, :]
        meridional = 0.5 * north[l : l + 1, :]
        to_east = KAPPA_COEF - zonal
        to_west = KAPPA_COEF + zonal
        to_north = jnp.where(lane == rows - 1, 0.0, KAPPA_COEF - meridional)
        to_south = jnp.where(lane == 0, 0.0, KAPPA_COEF + meridional)

        def step(west, here, east_):
            total = None
            if here is not None:
                total = (
                    (1.0 - 4.0 * KAPPA_COEF) * here
                    + to_north * pltpu.roll(here, rows - 1, 1)
                    + to_south * pltpu.roll(here, 1, 1)
                )
            if east_ is not None:
                total = to_east * east_ if total is None else total + to_east * east_
            if west is not None:
                total = to_west * west if total is None else total + to_west * west
            return total

        none = [None] * reach
        start = none + [plain[g * columns + k] for k in range(columns)] + none
        once = [None] * span
        for k in range(1, span - 1):
            value = step(start[k - 1], start[k], start[k + 1])
            if k < reach or k >= reach + columns:
                col = first + (k - reach)
                inside = jnp.logical_and(col >= 0, col < total_cols)
                value = jnp.where(inside, value, 0.0)
            once[k] = value
        for k in range(span):
            west = once[k - 1] if k > 0 else None
            east_ = once[k + 1] if k < span - 1 else None
            value = step(west, once[k], east_)
            ahead[g * span + k] = value
            if k < reach:
                to_left[g * reach + k] = value
            elif k < reach + columns:
                grid[g * columns + k - reach] = value
            else:
                to_right[g * reach + k - reach - columns] = value
    for out in (mine, other):
        out[batches * members :, :] = jnp.zeros(
            (out.shape[0] - batches * members, LANES), jnp.float32
        )
    vt = jnp.zeros((8, LANES), jnp.float32)
    spot = lax.broadcasted_iota(jnp.int32, (8, LANES), 1)
    for k in range(table.shape[1]):
        own_weight = jnp.where(core == 0, table[0, k], table[1, k])
        vt = jnp.where(spot == k, own_weight, vt)
    mine[batches * members : batches * members + 8, :] = jnp.where(origin == 1, vt, 0.0)

    def pick(b, carry):
        rows_of = pl.ds(pl.multiple_of(b * members, 8), members)
        slot = cols[pl.ds(b, 1), :] - (first - reach)
        inside = jnp.logical_and(slot >= 0, slot < span)
        target = jnp.where(inside, flds[pl.ds(b, 1), :] * span + slot, -1)
        present = seen[b] > 0

        @pl.when(jnp.logical_not(present))
        def _():
            mine[rows_of, :] = jnp.zeros((members, LANES), jnp.float32)
            other[rows_of, :] = jnp.zeros((members, LANES), jnp.float32)

        @pl.when(present)
        def _():
            wanted = jnp.broadcast_to(target, (members, LANES))
            index = jnp.broadcast_to(rws[pl.ds(b, 1), :], (members, LANES))
            for out, level in ((mine, core), (other, 1 - core)):
                total = jnp.zeros((members, LANES), jnp.float32)
                for f in range(fields):
                    for k in range(span):
                        slab = ahead[(f * levels + level) * span + k]
                        picked = jnp.take_along_axis(slab, index, axis=1)
                        total = jnp.where(wanted == f * span + k, picked, total)
                out[rows_of, :] = total

        return carry

    lax.fori_loop(0, batches, pick, 0)


def halves(x):
    high = x.astype(jnp.bfloat16)
    low = (x - high.astype(jnp.float32)).astype(jnp.bfloat16)
    return high, low


def analysis_kernel(count, place, table, *refs):
    info, refs = refs[:5], refs[5:]
    arrived, rest = refs[:count], refs[count:]
    grid, from_left, from_right, out = rest[:4]
    local, remote, edges, spread_rows, spread_cols, vertical, position, sems = rest[4:]
    all_levels, length, _ = remote.shape
    slabs, members, rows = grid.shape
    fields, levels, columns = out.shape[1], out.shape[2], out.shape[3]
    groups = fields * levels
    batches = info[0].shape[0]
    total_cols = place[1].astype(jnp.float32)
    classes = table.shape[1]
    first = place[0].astype(jnp.float32)
    incoming = []
    level, at = 0, 0
    for ref in arrived:
        size = ref.shape[0]
        incoming.append((ref, remote.at[level, at : at + size]))
        at += size
        if at == length:
            level, at = level + 1, 0
    incoming += [(grid, local), (from_left, edges.at[0]), (from_right, edges.at[1])]
    incoming = [
        pltpu.make_async_copy(ref, target, sems.at[slabs + n])
        for n, (ref, target) in enumerate(incoming)
    ]
    for copy in incoming:
        copy.start()
    for copy in incoming:
        copy.wait()
    for g in range(groups):
        for k in range(2):
            west, east = g * columns + k, g * columns + columns - 2 + k
            local[west] = local[west] + edges[0, g * 2 + k]
            local[east] = local[east] + edges[1, g * 2 + k]
    inverse = 1.0 / total_cols

    def widen(x):
        high, low = halves(x)
        return jnp.concatenate([high, high, low], axis=0)

    def spread_out(turn, weighted):
        change = jnp.dot(
            spread_rows[turn],
            jnp.concatenate(halves(weighted), axis=0),
            preferred_element_type=jnp.float32,
        )
        return change[:members] + change[members:]

    def covariance(turn, x):
        return jnp.dot(spread_cols[turn], widen(x), preferred_element_type=jnp.float32)

    def update(turn, x, weight):
        return x + spread_out(turn, covariance(turn, x) * weight)

    def rows_of(c):
        return pl.ds(pl.multiple_of(c * members, 8), members)

    def fact(k, c):
        return info[k][pl.ds(c, 1), :].astype(jnp.float32)

    def taper_to(turn, c):
        d_col = (fact(0, c) - position[turn, 0]) * inverse
        d_row = (fact(1, c) - position[turn, 1]) * (1.0 / RADY)
        radial = jnp.maximum(1.0 - d_col * d_col - d_row * d_row, 0.0)
        return radial * radial

    def analyse(turn, c, total):
        priors = total * (1.0 / all_levels)
        average = jnp.sum(priors, axis=0, keepdims=True) * (1.0 / members)
        spread = priors - average
        variance = jnp.sum(spread * spread, axis=0, keepdims=True) / (members - 1) + EPSILON
        error = fact(4, c)
        ratio = 1.0 / (variance + error)
        shrink = variance * ratio
        factor = jnp.sqrt(error * ratio)
        increments = shrink * (fact(3, c) - average) + (factor - 1.0) * spread
        regress = spread / ((members - 1) * variance)
        high, low = halves(increments)
        spread_rows[turn, :members, :LANES] = high
        spread_rows[turn, :members, LANES:] = high
        spread_rows[turn, members:, :LANES] = low
        spread_rows[turn, members:, LANES:] = jnp.zeros_like(low)
        high = regress.astype(jnp.bfloat16).astype(jnp.float32)
        low = regress - high
        stacked = jnp.concatenate(
            [high, low, high, jnp.zeros((256 - 3 * members, LANES), jnp.float32)], axis=0
        )
        spread_cols[turn] = jnp.transpose(stacked)[:, : 3 * members].astype(jnp.bfloat16)

        def column_of(k):
            return jnp.transpose(jnp.broadcast_to(fact(k, c), (LANES, LANES)))

        position[turn, 0] = column_of(0)
        position[turn, 1] = column_of(1)
        obs_class = column_of(2)
        for level in range(all_levels + levels):
            if level < all_levels:
                row = remote[level, batches * members : batches * members + 8, :]
                weights = [
                    jnp.broadcast_to(row[0:1, k : k + 1], (LANES, LANES)) for k in range(classes)
                ]
            else:
                weights = [table[level - all_levels, k] for k in range(classes)]
            chosen = jnp.zeros((LANES, LANES), jnp.float32) + weights[classes - 1]
            for k in range(classes - 1):
                chosen = jnp.where(obs_class == float(k), weights[k], chosen)
            vertical[turn, level] = chosen

    def batch(b, carry):
        turn = b % 2
        soon = jnp.minimum(b + 1, batches - 1)
        xs = [remote[g, rows_of(soon), :] for g in range(all_levels)]
        linked = covariance(turn, jnp.concatenate(xs, axis=1))
        weighted = linked[:, :LANES] * vertical[turn, 0]
        total = xs[0]
        for g in range(1, all_levels):
            weighted = weighted + linked[:, g * LANES : (g + 1) * LANES] * vertical[turn, g]
            total = total + xs[g]
        total = total + spread_out(turn, weighted * taper_to(turn, soon))

        lane = lax.broadcasted_iota(jnp.int32, (1, LANES), 1).astype(jnp.float32)
        d_row = (lane - position[turn, 1]) * (1.0 / RADY)
        across = 1.0 - d_row * d_row
        along = (first - position[turn, 0]) * inverse
        ats, ws = [], []
        for k in range(columns):
            d_col = along + k * inverse
            radial = jnp.maximum(across - d_col * d_col, 0.0)
            taper = radial * radial
            for level in range(levels):
                weight = taper * vertical[turn, all_levels + level]
                for f in range(fields):
                    ats.append((f * levels + level) * columns + k)
                    ws.append(weight)
        x = jnp.concatenate([local[at] for at in ats], axis=1)
        x = update(turn, x, jnp.concatenate(ws, axis=1))
        for i, at in enumerate(ats):
            local[at] = x[:, i * LANES : (i + 1) * LANES]
        analyse(1 - turn, soon, total)

        def later_many(c0, many):
            xs, ws, keep = [], [], []
            for k in range(many):
                theirs = rows_of(c0 + k)
                taper = taper_to(turn, c0 + k)
                for g in range(all_levels):
                    xs.append(remote[g, theirs, :])
                    ws.append(taper * vertical[turn, g])
                    keep.append((g, theirs))
            x = update(turn, jnp.concatenate(xs, axis=1), jnp.concatenate(ws, axis=1))
            for n, (g, theirs) in enumerate(keep):
                remote[g, theirs, :] = x[:, n * LANES : (n + 1) * LANES]

        count = jnp.maximum(batches - 2 - b, 0)

        for size in (1, 2):

            @pl.when((count // size) % 2 == 1)
            def _():
                later_many(b + 2 + (count % size), size)

        start = b + 2 + count % 4

        def four(i, carry):
            later_many(start + 4 * i, 4)
            return carry

        lax.fori_loop(0, count // 4, four, 0)
        return carry

    total = remote[0, 0:members, :]
    for level in range(1, all_levels):
        total = total + remote[level, 0:members, :]
    analyse(0, 0, total)
    lax.fori_loop(0, batches, batch, 0)
    outgoing = []
    for f in range(fields):
        for level in range(levels):
            for k in range(columns):
                at = (f * levels + level) * columns + k
                outgoing.append(
                    pltpu.make_async_copy(
                        local.at[at], out.at[:, f, level, k, :], sems.at[at]
                    )
                )
    for copy in outgoing:
        copy.start()
    for copy in outgoing:
        copy.wait()


def forecast(place, table, state, east, north, cols, rws, flds, length):
    members, fields, levels, columns, rows = state.shape
    groups = fields * levels
    smem = pl.BlockSpec(memory_space=pltpu.SMEM)
    vmem = pl.BlockSpec(memory_space=pltpu.VMEM)
    anywhere = pl.BlockSpec(memory_space=pl.ANY)
    picks = jax.ShapeDtypeStruct((length, LANES), jnp.float32)
    edge = jax.ShapeDtypeStruct((groups * 2, members, rows), jnp.float32)
    return pl.pallas_call(
        forecast_kernel,
        out_shape=(
            jax.ShapeDtypeStruct((groups * columns, members, rows), jnp.float32),
            edge,
            edge,
            picks,
            picks,
        ),
        in_specs=[smem, smem, anywhere] + [vmem] * 5,
        out_specs=(vmem,) * 5,
        scratch_shapes=[
            pltpu.VMEM((groups * columns, members, rows), jnp.float32),
            pltpu.VMEM((groups * (columns + 4), members, rows), jnp.float32),
            pltpu.SMEM((cols.shape[0],), jnp.int32),
            pltpu.SemaphoreType.DMA((groups * columns,)),
        ],
        compiler_params=pltpu.CompilerParams(vmem_limit_bytes=40 * 2**20),
    )(place, table, state, east, north, cols, rws, flds)


def assimilate(place, table, info, arrived, grid, from_left, from_right, shape, length):
    members, fields, levels, columns, rows = shape
    smem = pl.BlockSpec(memory_space=pltpu.SMEM)
    vmem = pl.BlockSpec(memory_space=pltpu.VMEM)
    anywhere = pl.BlockSpec(memory_space=pl.ANY)
    all_levels = sum(part.shape[0] for part in arrived) // length
    return pl.pallas_call(
        functools.partial(analysis_kernel, len(arrived)),
        out_shape=jax.ShapeDtypeStruct(shape, jnp.float32),
        in_specs=[smem, smem] + [vmem] * len(info) + [anywhere] * (len(arrived) + 3),
        out_specs=anywhere,
        scratch_shapes=[
            pltpu.VMEM(grid.shape, jnp.float32),
            pltpu.VMEM((all_levels, length, LANES), jnp.float32),
            pltpu.VMEM((2,) + from_left.shape, jnp.float32),
            pltpu.VMEM((2, 2 * members, 2 * LANES), jnp.bfloat16),
            pltpu.VMEM((2, LANES, 3 * members), jnp.bfloat16),
            pltpu.VMEM((2, all_levels + levels, LANES, LANES), jnp.float32),
            pltpu.VMEM((2, 2, LANES, LANES), jnp.float32),
            pltpu.SemaphoreType.DMA((grid.shape[0] + len(arrived) + 3,)),
        ],
        compiler_params=pltpu.CompilerParams(vmem_limit_bytes=60 * 2**20),
    )(place, table, *info, *arrived, grid, from_left, from_right)


def shards(
    state,
    eastward_current,
    northward_current,
    obs_col,
    obs_row,
    obs_field,
    obs_class,
    obs_value,
    obs_error,
    vertical_table,
):
    members, fields, levels, columns, rows = state.shape
    batches, obs = obs_col.shape
    homes = lax.axis_size("z") * lax.axis_size("y")
    tiles = homes * lax.axis_size("core")
    tile = lax.axis_index(TILES)
    core = lax.axis_index("core")
    first = tile * columns
    chunk = -(-(batches * members + 8) // (8 * homes)) * 8
    length = chunk * homes

    table = vertical_table.T
    origin = (tile // 2 == 0).astype(jnp.int32)
    place = jnp.stack([first, core, origin, jnp.int32(tiles * columns)]).astype(jnp.int32)
    grid, to_left, to_right, mine, other = forecast(
        place, table, state, eastward_current, northward_current, obs_col, obs_row,
        obs_field, length,
    )

    swap = [(0, 1), (1, 0)]
    mine = mine + lax.ppermute(other, "core", swap)
    mine = lax.all_to_all(mine.reshape(homes, chunk, LANES), ("z", "y"), 0, 0, tiled=True)
    mine = jnp.sum(mine, axis=0)
    mine = lax.all_to_all(
        jnp.broadcast_to(mine[None], (homes, chunk, LANES)), ("z", "y"), 0, 0, tiled=True
    )
    mine = mine.reshape(length, LANES)

    ring = lax.axis_size("x")
    right = [(i, (i + 1) % ring) for i in range(ring)]
    left = [(j, i) for i, j in right]
    up = [(i, i + 1) for i in range(tiles - 1)]
    down = [(j, i) for i, j in up]
    used = batches * members + 8
    middle = used // 16 * 8
    mine, to_left, to_right = lax.optimization_barrier((mine[:used], to_left, to_right))
    before = lax.ppermute(mine, "x", right)
    after = lax.ppermute(mine, "x", left)
    from_left = lax.ppermute(to_right, TILES, up)
    from_right = lax.ppermute(to_left, TILES, down)
    across_a = lax.ppermute(after[:middle], "x", left)
    across_b = lax.ppermute(before[middle:], "x", right)
    parts = [mine, before, after, across_a, across_b]
    arrived = parts + [lax.ppermute(part, "core", swap) for part in parts]

    facts = [obs_col, obs_row, obs_class, obs_value, obs_error]
    where = jnp.stack([first, jnp.int32(tiles * columns)]).astype(jnp.int32)
    return assimilate(
        where, table, facts, arrived, grid, from_left, from_right, state.shape, used
    )


def solution(mesh):
    fine = Mesh(mesh.devices.reshape(8, 8, 2, 4), ("z", "y", "core", "x"))
    state = P(None, None, "x", TILES, None)
    placed = (
        state,
        P("x", None),
        P("x", None),
        P(),
        P(),
        P(),
        P(),
        P(),
        P(),
        P(None, "x"),
    )
    return jax.shard_map(shards, mesh=fine, in_specs=placed, out_specs=state, check_vma=False)
```

```python
import functools

import jax
import jax.numpy as jnp
from jax import lax
from jax.experimental import pallas as pl
from jax.experimental.pallas import tpu as pltpu
from jax.sharding import Mesh, PartitionSpec as P

RADY = 40
KAPPA_COEF = 0.2
EPSILON = 1e-05
LANES = 128
TILES = ("z", "y", "core")


def forecast_kernel(
    place, table, state, east, north, cols, rws, flds, grid, to_left, to_right, mine, other,
    plain, ahead, seen, sems
):
    members, fields, levels, columns, rows = state.shape
    reach = 2
    batches = cols.shape[0]
    span = columns + 2 * reach
    groups = fields * levels
    first, core, origin, total_cols = place[0], place[1], place[2], place[3]
    copies = []
    for g in range(groups):
        for k in range(columns):
            slot = g * columns + k
            copies.append(
                pltpu.make_async_copy(
                    state.at[:, g // levels, g % levels, k, :], plain.at[slot], sems.at[slot]
                )
            )
    for copy in copies:
        copy.start()
    slot = cols[...] - (first - reach)
    near = jnp.where(jnp.logical_and(slot >= 0, slot < span), 1.0, 0.0)
    near = jnp.max(near, axis=1, keepdims=True)
    for b in range(batches):
        seen[b] = near[b, 0].astype(jnp.int32)
    lane = lax.broadcasted_iota(jnp.int32, (1, rows), 1)
    for g in range(groups):
        for k in range(columns):
            copies[g * columns + k].wait()
        l = g % levels
        zonal = 0.5 * east[l : l + 1, :]
        meridional = 0.5 * north[l : l + 1, :]
        to_east = KAPPA_COEF - zonal
        to_west = KAPPA_COEF + zonal
        to_north = jnp.where(lane == rows - 1, 0.0, KAPPA_COEF - meridional)
        to_south = jnp.where(lane == 0, 0.0, KAPPA_COEF + meridional)

        def step(west, here, east_):
            total = None
            if here is not None:
                total = (
                    (1.0 - 4.0 * KAPPA_COEF) * here
                    + to_north * pltpu.roll(here, rows - 1, 1)
                    + to_south * pltpu.roll(here, 1, 1)
                )
            if east_ is not None:
                total = to_east * east_ if total is None else total + to_east * east_
            if west is not None:
                total = to_west * west if total is None else total + to_west * west
            return total

        none = [None] * reach
        start = none + [plain[g * columns + k] for k in range(columns)] + none
        once = [None] * span
        for k in range(1, span - 1):
            value = step(start[k - 1], start[k], start[k + 1])
            if k < reach or k >= reach + columns:
                col = first + (k - reach)
                inside = jnp.logical_and(col >= 0, col < total_cols)
                value = jnp.where(inside, value, 0.0)
            once[k] = value
        for k in range(span):
            west = once[k - 1] if k > 0 else None
            east_ = once[k + 1] if k < span - 1 else None
            value = step(west, once[k], east_)
            ahead[g * span + k] = value
            if k < reach:
                to_left[g * reach + k] = value
            elif k < reach + columns:
                grid[g * columns + k - reach] = value
            else:
                to_right[g * reach + k - reach - columns] = value
    for out in (mine, other):
        out[batches * members :, :] = jnp.zeros(
            (out.shape[0] - batches * members, LANES), jnp.float32
        )
    vt = jnp.zeros((8, LANES), jnp.float32)
    spot = lax.broadcasted_iota(jnp.int32, (8, LANES), 1)
    for k in range(table.shape[1]):
        own_weight = jnp.where(core == 0, table[0, k], table[1, k])
        vt = jnp.where(spot == k, own_weight, vt)
    mine[batches * members : batches * members + 8, :] = jnp.where(origin == 1, vt, 0.0)

    def pick(b, carry):
        rows_of = pl.ds(pl.multiple_of(b * members, 8), members)
        slot = cols[pl.ds(b, 1), :] - (first - reach)
        inside = jnp.logical_and(slot >= 0, slot < span)
        target = jnp.where(inside, flds[pl.ds(b, 1), :] * span + slot, -1)
        present = seen[b] > 0

        @pl.when(jnp.logical_not(present))
        def _():
            mine[rows_of, :] = jnp.zeros((members, LANES), jnp.float32)
            other[rows_of, :] = jnp.zeros((members, LANES), jnp.float32)

        @pl.when(present)
        def _():
            wanted = jnp.broadcast_to(target, (members, LANES))
            index = jnp.broadcast_to(rws[pl.ds(b, 1), :], (members, LANES))
            for out, level in ((mine, core), (other, 1 - core)):
                total = jnp.zeros((members, LANES), jnp.float32)
                for f in range(fields):
                    for k in range(span):
                        slab = ahead[(f * levels + level) * span + k]
                        picked = jnp.take_along_axis(slab, index, axis=1)
                        total = jnp.where(wanted == f * span + k, picked, total)
                out[rows_of, :] = total

        return carry

    lax.fori_loop(0, batches, pick, 0)


def halves(x):
    high = x.astype(jnp.bfloat16)
    low = (x - high.astype(jnp.float32)).astype(jnp.bfloat16)
    return high, low


def analysis_kernel(count, place, table, *refs):
    info, refs = refs[:5], refs[5:]
    arrived, rest = refs[:count], refs[count:]
    grid, from_left, from_right, out = rest[:4]
    local, remote, edges, spread_rows, spread_cols, vertical, position, sems = rest[4:]
    all_levels, length, _ = remote.shape
    slabs, members, rows = grid.shape
    fields, levels, columns = out.shape[1], out.shape[2], out.shape[3]
    groups = fields * levels
    batches = info[0].shape[0]
    total_cols = place[1].astype(jnp.float32)
    classes = table.shape[1]
    first = place[0].astype(jnp.float32)
    incoming = []
    level, at = 0, 0
    for ref in arrived:
        size = ref.shape[0]
        incoming.append((ref, remote.at[level, at : at + size]))
        at += size
        if at == length:
            level, at = level + 1, 0
    incoming += [(grid, local), (from_left, edges.at[0]), (from_right, edges.at[1])]
    incoming = [
        pltpu.make_async_copy(ref, target, sems.at[slabs + n])
        for n, (ref, target) in enumerate(incoming)
    ]
    for copy in incoming:
        copy.start()
    for copy in incoming:
        copy.wait()
    for g in range(groups):
        for k in range(2):
            west, east = g * columns + k, g * columns + columns - 2 + k
            local[west] = local[west] + edges[0, g * 2 + k]
            local[east] = local[east] + edges[1, g * 2 + k]
    inverse = 1.0 / total_cols

    def widen(x):
        high, low = halves(x)
        return jnp.concatenate([high, high, low], axis=0)

    def spread_out(turn, weighted):
        change = jnp.dot(
            spread_rows[turn],
            jnp.concatenate(halves(weighted), axis=0),
            preferred_element_type=jnp.float32,
        )
        return change[:members] + change[members:]

    def covariance(turn, x):
        return jnp.dot(spread_cols[turn], widen(x), preferred_element_type=jnp.float32)

    def update(turn, x, weight):
        return x + spread_out(turn, covariance(turn, x) * weight)

    def rows_of(c):
        return pl.ds(pl.multiple_of(c * members, 8), members)

    def fact(k, c):
        return info[k][pl.ds(c, 1), :].astype(jnp.float32)

    def taper_to(turn, c):
        d_col = (fact(0, c) - position[turn, 0]) * inverse
        d_row = (fact(1, c) - position[turn, 1]) * (1.0 / RADY)
        radial = jnp.maximum(1.0 - d_col * d_col - d_row * d_row, 0.0)
        return radial * radial

    def analyse(turn, c, total):
        priors = total * (1.0 / all_levels)
        average = jnp.sum(priors, axis=0, keepdims=True) * (1.0 / members)
        spread = priors - average
        variance = jnp.sum(spread * spread, axis=0, keepdims=True) / (members - 1) + EPSILON
        error = fact(4, c)
        ratio = 1.0 / (variance + error)
        shrink = variance * ratio
        factor = jnp.sqrt(error * ratio)
        increments = shrink * (fact(3, c) - average) + (factor - 1.0) * spread
        regress = spread / ((members - 1) * variance)
        high, low = halves(increments)
        spread_rows[turn, :members, :LANES] = high
        spread_rows[turn, :members, LANES:] = high
        spread_rows[turn, members:, :LANES] = low
        spread_rows[turn, members:, LANES:] = jnp.zeros_like(low)
        high = regress.astype(jnp.bfloat16).astype(jnp.float32)
        low = regress - high
        stacked = jnp.concatenate(
            [high, low, high, jnp.zeros((256 - 3 * members, LANES), jnp.float32)], axis=0
        )
        spread_cols[turn] = jnp.transpose(stacked)[:, : 3 * members].astype(jnp.bfloat16)

        def column_of(k):
            return jnp.transpose(jnp.broadcast_to(fact(k, c), (LANES, LANES)))

        position[turn, 0] = column_of(0)
        position[turn, 1] = column_of(1)
        obs_class = column_of(2)
        for level in range(all_levels + levels):
            if level < all_levels:
                row = remote[level, batches * members : batches * members + 8, :]
                weights = [
                    jnp.broadcast_to(row[0:1, k : k + 1], (LANES, LANES)) for k in range(classes)
                ]
            else:
                weights = [table[level - all_levels, k] for k in range(classes)]
            chosen = jnp.zeros((LANES, LANES), jnp.float32) + weights[classes - 1]
            for k in range(classes - 1):
                chosen = jnp.where(obs_class == float(k), weights[k], chosen)
            vertical[turn, level] = chosen

    def batch(b, carry):
        turn = b % 2
        soon = jnp.minimum(b + 1, batches - 1)
        xs = [remote[g, rows_of(soon), :] for g in range(all_levels)]
        linked = covariance(turn, jnp.concatenate(xs, axis=1))
        weighted = linked[:, :LANES] * vertical[turn, 0]
        total = xs[0]
        for g in range(1, all_levels):
            weighted = weighted + linked[:, g * LANES : (g + 1) * LANES] * vertical[turn, g]
            total = total + xs[g]
        total = total + spread_out(turn, weighted * taper_to(turn, soon))

        lane = lax.broadcasted_iota(jnp.int32, (1, LANES), 1).astype(jnp.float32)
        d_row = (lane - position[turn, 1]) * (1.0 / RADY)
        across = 1.0 - d_row * d_row
        along = (first - position[turn, 0]) * inverse
        ats, ws = [], []
        for k in range(columns):
            d_col = along + k * inverse
            radial = jnp.maximum(across - d_col * d_col, 0.0)
            taper = radial * radial
            for level in range(levels):
                weight = taper * vertical[turn, all_levels + level]
                for f in range(fields):
                    ats.append((f * levels + level) * columns + k)
                    ws.append(weight)
        x = jnp.concatenate([local[at] for at in ats], axis=1)
        x = update(turn, x, jnp.concatenate(ws, axis=1))
        for i, at in enumerate(ats):
            local[at] = x[:, i * LANES : (i + 1) * LANES]
        analyse(1 - turn, soon, total)

        def later_many(c0, many):
            xs, ws, keep = [], [], []
            for k in range(many):
                theirs = rows_of(c0 + k)
                taper = taper_to(turn, c0 + k)
                for g in range(all_levels):
                    xs.append(remote[g, theirs, :])
                    ws.append(taper * vertical[turn, g])
                    keep.append((g, theirs))
            x = update(turn, jnp.concatenate(xs, axis=1), jnp.concatenate(ws, axis=1))
            for n, (g, theirs) in enumerate(keep):
                remote[g, theirs, :] = x[:, n * LANES : (n + 1) * LANES]

        count = jnp.maximum(batches - 2 - b, 0)

        for size in (1, 2):

            @pl.when((count // size) % 2 == 1)
            def _():
                later_many(b + 2 + (count % size), size)

        start = b + 2 + count % 4

        def four(i, carry):
            later_many(start + 4 * i, 4)
            return carry

        lax.fori_loop(0, count // 4, four, 0)
        return carry

    total = remote[0, 0:members, :]
    for level in range(1, all_levels):
        total = total + remote[level, 0:members, :]
    analyse(0, 0, total)
    lax.fori_loop(0, batches, batch, 0)
    outgoing = []
    for f in range(fields):
        for level in range(levels):
            for k in range(columns):
                at = (f * levels + level) * columns + k
                outgoing.append(
                    pltpu.make_async_copy(
                        local.at[at], out.at[:, f, level, k, :], sems.at[at]
                    )
                )
    for copy in outgoing:
        copy.start()
    for copy in outgoing:
        copy.wait()


def forecast(place, table, state, east, north, cols, rws, flds, length):
    members, fields, levels, columns, rows = state.shape
    groups = fields * levels
    smem = pl.BlockSpec(memory_space=pltpu.SMEM)
    vmem = pl.BlockSpec(memory_space=pltpu.VMEM)
    anywhere = pl.BlockSpec(memory_space=pl.ANY)
    picks = jax.ShapeDtypeStruct((length, LANES), jnp.float32)
    edge = jax.ShapeDtypeStruct((groups * 2, members, rows), jnp.float32)
    return pl.pallas_call(
        forecast_kernel,
        out_shape=(
            jax.ShapeDtypeStruct((groups * columns, members, rows), jnp.float32),
            edge,
            edge,
            picks,
            picks,
        ),
        in_specs=[smem, smem, anywhere] + [vmem] * 5,
        out_specs=(vmem,) * 5,
        scratch_shapes=[
            pltpu.VMEM((groups * columns, members, rows), jnp.float32),
            pltpu.VMEM((groups * (columns + 4), members, rows), jnp.float32),
            pltpu.SMEM((cols.shape[0],), jnp.int32),
            pltpu.SemaphoreType.DMA((groups * columns,)),
        ],
        compiler_params=pltpu.CompilerParams(vmem_limit_bytes=40 * 2**20),
    )(place, table, state, east, north, cols, rws, flds)


def assimilate(place, table, info, arrived, grid, from_left, from_right, shape, length):
    members, fields, levels, columns, rows = shape
    smem = pl.BlockSpec(memory_space=pltpu.SMEM)
    vmem = pl.BlockSpec(memory_space=pltpu.VMEM)
    anywhere = pl.BlockSpec(memory_space=pl.ANY)
    all_levels = sum(part.shape[0] for part in arrived) // length
    return pl.pallas_call(
        functools.partial(analysis_kernel, len(arrived)),
        out_shape=jax.ShapeDtypeStruct(shape, jnp.float32),
        in_specs=[smem, smem] + [vmem] * len(info) + [anywhere] * (len(arrived) + 3),
        out_specs=anywhere,
        scratch_shapes=[
            pltpu.VMEM(grid.shape, jnp.float32),
            pltpu.VMEM((all_levels, length, LANES), jnp.float32),
            pltpu.VMEM((2,) + from_left.shape, jnp.float32),
            pltpu.VMEM((2, 2 * members, 2 * LANES), jnp.bfloat16),
            pltpu.VMEM((2, LANES, 3 * members), jnp.bfloat16),
            pltpu.VMEM((2, all_levels + levels, LANES, LANES), jnp.float32),
            pltpu.VMEM((2, 2, LANES, LANES), jnp.float32),
            pltpu.SemaphoreType.DMA((grid.shape[0] + len(arrived) + 3,)),
        ],
        compiler_params=pltpu.CompilerParams(vmem_limit_bytes=60 * 2**20),
    )(place, table, *info, *arrived, grid, from_left, from_right)


def shards(
    state,
    eastward_current,
    northward_current,
    obs_col,
    obs_row,
    obs_field,
    obs_class,
    obs_value,
    obs_error,
    vertical_table,
):
    members, fields, levels, columns, rows = state.shape
    batches, obs = obs_col.shape
    homes = lax.axis_size("z") * lax.axis_size("y")
    tiles = homes * lax.axis_size("core")
    tile = lax.axis_index(TILES)
    core = lax.axis_index("core")
    first = tile * columns
    chunk = -(-(batches * members + 8) // (8 * homes)) * 8
    length = chunk * homes

    table = vertical_table.T
    origin = (tile // 2 == 0).astype(jnp.int32)
    place = jnp.stack([first, core, origin, jnp.int32(tiles * columns)]).astype(jnp.int32)
    grid, to_left, to_right, mine, other = forecast(
        place, table, state, eastward_current, northward_current, obs_col, obs_row,
        obs_field, length,
    )

    swap = [(0, 1), (1, 0)]
    mine = mine + lax.ppermute(other, "core", swap)
    mine = lax.all_to_all(mine.reshape(homes, chunk, LANES), ("z", "y"), 0, 0, tiled=True)
    mine = jnp.sum(mine, axis=0)
    mine = lax.all_to_all(
        jnp.broadcast_to(mine[None], (homes, chunk, LANES)), ("z", "y"), 0, 0, tiled=True
    )
    mine = mine.reshape(length, LANES)

    ring = lax.axis_size("x")
    right = [(i, (i + 1) % ring) for i in range(ring)]
    left = [(j, i) for i, j in right]
    up = [(i, i + 1) for i in range(tiles - 1)]
    down = [(j, i) for i, j in up]
    used = batches * members + 8
    middle = used // 16 * 8
    mine, to_left, to_right = lax.optimization_barrier((mine[:used], to_left, to_right))
    before = lax.ppermute(mine, "x", right)
    after = lax.ppermute(mine, "x", left)
    from_left = lax.ppermute(to_right, TILES, up)
    from_right = lax.ppermute(to_left, TILES, down)
    across_a = lax.ppermute(after[:middle], "x", left)
    across_b = lax.ppermute(before[middle:], "x", right)
    mine, before, after, across_a = lax.optimization_barrier((mine, before, after, across_a))
    parts = [mine, before, after, across_a, across_b]
    arrived = parts + [lax.ppermute(part, "core", swap) for part in parts]

    facts = [obs_col, obs_row, obs_class, obs_value, obs_error]
    where = jnp.stack([first, jnp.int32(tiles * columns)]).astype(jnp.int32)
    return assimilate(
        where, table, facts, arrived, grid, from_left, from_right, state.shape, used
    )


def solution(mesh):
    fine = Mesh(mesh.devices.reshape(8, 8, 2, 4), ("z", "y", "core", "x"))
    state = P(None, None, "x", TILES, None)
    placed = (
        state,
        P("x", None),
        P("x", None),
        P(),
        P(),
        P(),
        P(),
        P(),
        P(),
        P(None, "x"),
    )
    return jax.shard_map(shards, mesh=fine, in_specs=placed, out_specs=state, check_vma=False)
```
